32 devices in a mesh: groups: 2 (over y), cls: 16 (over z, x, core).
Axes of the slice: x: 2, y: 2, z: 4, core: 2. Of those that a mesh axis runs over, the one named last changes fastest.
Arguments:
- particle_tiles: bfloat16 [768, 256, 256], P(('groups', 'cls')), parts along dimension 0, may hold values from -30 to 30
- class_lists: int32 [768, 2], P(('groups', 'cls')), parts along dimension 0, may hold values from 0 to 15, all different within a row; in each aligned block of 24 rows (0 to 23, 24 to 47, ...) at most 6 rows name the same one
- offsets: int32 [768, 2], P(('groups', 'cls')), parts along dimension 0, may hold values from -8 to 8
- defocus_groups: int32 [768], P(('groups', 'cls')), parts along dimension 0, may hold values from 0 to 15
- contrast_table: bfloat16 [16, 128, 128], replicated, may hold values from -1 to 1
- references: float32 [32, 2, 128, 128], P(('groups', 'cls')), parts along dimension 0, may hold values from -30 to 30
- rotations: bfloat16 [12, 128, 128], replicated, may hold values from -0.5 to 0.5
Outputs:
- class_numerators: float32 [32, 2, 128, 128], P(('groups', 'cls')), parts along dimension 0
- log_evidence: float32 [768, 2], P(('groups', 'cls')), parts along dimension 0
The draws below stay inside these ranges and needn't reach their ends.
There are 2 independent parts, one for each index of `groups`. The reference program is written for one: setup_inputs(seed, part) draws one part's arguments, and reference() takes and returns one part's arrays. A program takes and returns all parts, laid end to end along the dimension named above; an argument that names none is the same for every part. Nothing has to cross between parts.
Inputs may be any that keep to these rules, and one draw needn't show every extreme that they name: `class_lists`: among the entries of the particles of one device no class is named more than 6 times, a bound that some block reaches. Every class is named by some particle; the two classes of a particle differ.
All inputs are finite; a program needn't handle non-finite values.
Results may differ from the reference program's by a relative error of at most 0.015.
The reference program's roundings to bfloat16 on the way count: a program that leaves them out, or rounds other values in their place, can miss the bound.
Values may be sent and summed in bfloat16 or wider, within the bound.
No kernel may reach another device: no remote copies, remote signals or barrier semaphores. Data moves between devices by JAX's collectives and lax.ppermute only.
A program may use at most 128 MiB of HBM per device.

```python
import math
import jax
import jax.numpy as jnp
import numpy as np
from jax import lax

BOX = 256
BAND = 128
ROT = 12
TRANS = 9
TOP = 2
GRP = 16
P_DEV = 24
PARTICLES = 384
K = 16
CAP = 6
N_CLS = 16


def draw_particle_tiles(key, part):
    key = jax.random.fold_in(key, 11)
    noise_key, row_key, column_key = jax.random.split(key, 3)
    full_shape = (PARTICLES, BOX, BOX)
    row_scale = jnp.exp(jax.random.uniform(row_key, (PARTICLES, BOX, 1), jnp.float32, -1.15, 1.15))
    column_scale = jnp.exp(jax.random.uniform(column_key, (PARTICLES, 1, BOX), jnp.float32, -1.15, 1.15))
    noise_field = jnp.clip(jax.random.normal(noise_key, full_shape, jnp.float32), -3.0, 3.0)
    return (noise_field * row_scale * column_scale).astype(jnp.bfloat16)


def draw_references(key, part):
    key = jax.random.fold_in(key, 23)
    noise_key, row_key, column_key = jax.random.split(key, 3)
    full_shape = (K, 2, BAND, BAND)
    row_scale = jnp.exp(jax.random.uniform(row_key, (K, 2, BAND, 1), jnp.float32, -1.15, 1.15))
    column_scale = jnp.exp(jax.random.uniform(column_key, (K, 2, 1, BAND), jnp.float32, -1.15, 1.15))
    noise_field = jnp.clip(jax.random.normal(noise_key, full_shape, jnp.float32), -3.0, 3.0)
    return noise_field * row_scale * column_scale


def touch_ends(drawn, own_key, smallest, high):
    longest = drawn.shape.index(max(drawn.shape))
    spots = []
    for shift in (0, 1):
        where = [jax.random.randint(jax.random.fold_in(own_key, axis), (), 0, length) for axis, length in enumerate(drawn.shape)]
        where[longest] = (where[longest] + shift) % drawn.shape[longest]
        spots.append(tuple(where))
    return drawn.at[spots[0]].set(smallest).at[spots[1]].set(high)


def deal_out(stream_key, own, number, rows, count, top, most, slope):
    sequence = jax.random.permutation(stream_key, count)
    packed, ordinary = portions_of(count, rows * top, most, slope, True), portions_of(count, rows * top, most, slope, False)
    places = jnp.arange(count)

    def named(sizes, rotation):
        used = int((sizes > 0).sum())
        fixed = max(1, used // 4)
        passed = fixed + (places - fixed + rotation * (used - fixed)) % max(1, count - fixed)
        return jnp.zeros((count,), jnp.int32).at[sequence[jnp.where(places < fixed, places, passed)]].set(jnp.asarray(sizes, jnp.int32))

    sizes = jnp.where(number % 4 == 0, named(packed, number // 4), named(ordinary, number - number // 4 - 1))
    mixed = jax.random.permutation(jax.random.fold_in(own, 3), count)
    source_of, receiver = mixed[0:count // 2 * 2:2], mixed[1:count // 2 * 2:2]
    slack = jnp.minimum(sizes[source_of] - 1, most - sizes[receiver]) // 2
    slack = jnp.where((source_of == sequence[0]) | (receiver == sequence[0]) | (sizes[receiver] == 0), 0, jnp.maximum(slack, 0))
    passed = jax.random.randint(jax.random.fold_in(own, 4), (count // 2,), 0, 1 << 20) % (slack + 1)
    sizes = sizes.at[source_of].add(-passed).at[receiver].add(passed)
    items = jnp.searchsorted(jnp.cumsum(sizes), jnp.arange(rows * top), side="right").astype(jnp.int32)
    listing = items.reshape(top, rows).T
    listing = listing[jax.random.permutation(jax.random.fold_in(own, 1), rows)]
    rotation = jax.random.randint(jax.random.fold_in(own, 2), (rows, 1), 0, top)
    return jnp.take_along_axis(listing, (jnp.arange(top)[None, :] + rotation) % top, axis=1)


def portions_of(count, total, limit, skew, full):
    loads = [(1 << 20) // math.isqrt(rank ** skew) + 1 for rank in range(1, count + 1)]
    largest = limit if full else min(limit, max(-(-total // count), total * loads[0] // sum(loads)))
    least = 1 if total - largest >= count - 1 else 0
    given, spare = [largest] + [least] * (count - 1), total - largest - least * (count - 1)
    while spare > 0:
        free = [i for i in range(1, count) if given[i] < largest] or [i for i in range(1, count) if given[i] < limit]
        whole, left = sum([loads[i] for i in free]), spare
        for i in free:
            more = min(limit - given[i], max(1, left * loads[i] // whole), spare)
            given[i] = given[i] + more
            spare = spare - more
    return np.array(given)


def scatter_about(key, shape, spread, reach, kind=jnp.bfloat16):
    result = jax.random.normal(key, shape, jnp.float32) * spread
    return jnp.minimum(jnp.maximum(result, -reach), reach).astype(kind)


def setup_inputs(seed: int = 0, part: int = 0) -> dict:
    key_list = jax.random.split(jax.random.key(seed), 8)
    part_keys = jax.random.split(jax.random.fold_in(key_list[7], part), 8)
    particle_tiles = draw_particle_tiles(jax.random.fold_in(jax.random.fold_in(key_list[7], part), 71), part)
    class_lists_keys = jax.random.split(jax.random.fold_in(part_keys[1], 1), PARTICLES // P_DEV)
    class_lists_turns = jax.random.permutation(jax.random.fold_in(part_keys[1], 3), PARTICLES // P_DEV)
    class_lists = jax.vmap(lambda own, number: deal_out(jax.random.fold_in(part_keys[1], 2), own, number, P_DEV, K, TOP, CAP, 2))(class_lists_keys, class_lists_turns).reshape((PARTICLES, TOP))
    offsets = touch_ends(jax.random.randint(part_keys[2], (PARTICLES, 2), -8, 9), jax.random.fold_in(part_keys[2], 1), -8, 8).astype(jnp.int32)
    defocus_groups = touch_ends(jax.random.randint(part_keys[3], (PARTICLES,), 0, GRP), jax.random.fold_in(part_keys[3], 1), 0, GRP - 1).astype(jnp.int32)
    contrast_table = jnp.clip(jax.random.uniform(key_list[4], (GRP, BAND, BAND), jnp.float32, -1.0, 1.0), -1.0, 1.0).astype(jnp.bfloat16)
    references = draw_references(jax.random.fold_in(jax.random.fold_in(key_list[7], part), 71), part)
    rotations = scatter_about(key_list[6], (ROT, BAND, BAND), BAND ** -0.5, 0.5)
    return {"particle_tiles": particle_tiles, "class_lists": class_lists, "offsets": offsets, "defocus_groups": defocus_groups, "contrast_table": contrast_table, "references": references, "rotations": rotations}


SHIFT_GRID = ((-1, -1), (-1, 0), (-1, 1), (0, -1), (0, 0), (0, 1), (1, -1), (1, 0), (1, 1))

def frequencies(band):
    counter = jnp.arange(band, dtype=jnp.int32)
    return jnp.where(counter < band // 2, counter, counter - band)

def fourier_tables(box, band):
    frequency = frequencies(band)
    pixels = jnp.arange(box, dtype=jnp.int32)
    residue = frequency[:, None] * pixels[None, :] % box
    angles = residue.astype(jnp.float32) * (2.0 * math.pi / box)
    norm_factor = 1.0 / math.sqrt(box)
    cosine = (jnp.cos(angles) * norm_factor).astype(jnp.bfloat16)
    sine_part = (jnp.sin(angles) * norm_factor).astype(jnp.bfloat16)
    return jnp.concatenate([cosine, sine_part], 0)

def band_spectra(particle_tiles, stacked, band):
    first_pass = jnp.einsum('pxy,my->pxm', particle_tiles.astype(jnp.float32), stacked.astype(jnp.float32)).astype(jnp.bfloat16)
    second = jnp.einsum('jx,pxm->pjm', stacked.astype(jnp.float32), first_pass.astype(jnp.float32))
    real_part = second[:, :band, :band] - second[:, band:, band:]
    imag_part = -(second[:, band:, :band] + second[:, :band, band:])
    return jnp.stack([real_part, imag_part], 1).astype(jnp.bfloat16)

def phase_angles(shift_rows, shift_cols, band, box):
    frequency = frequencies(band)
    residue = (frequency[:, None] * shift_rows[..., None, None] + frequency[None, :] * shift_cols[..., None, None]) % box
    return residue.astype(jnp.float32) * (2.0 * math.pi / box)

def filtered(spectrum, contrast, offsets, band, box):
    angles = phase_angles(offsets[..., 0], offsets[..., 1], band, box)
    cosine = jnp.cos(angles)
    sine_part = jnp.sin(angles)
    contrast_gain = contrast.astype(jnp.float32)
    real_in = spectrum[..., 0, :, :].astype(jnp.float32)
    imag_in = spectrum[..., 1, :, :].astype(jnp.float32)
    real_out = contrast_gain * (cosine * real_in - sine_part * imag_in)
    imag_out = contrast_gain * (cosine * imag_in + sine_part * real_in)
    return jnp.stack([real_out, imag_out], -3).astype(jnp.bfloat16)

def grid_phases(band, box):
    shifts = jnp.array(SHIFT_GRID, dtype=jnp.int32)
    angles = phase_angles(shifts[:, 0], shifts[:, 1], band, box)
    return (jnp.cos(angles), jnp.sin(angles))

def templates(reference, rotations, band, box):
    reference_low = reference.astype(jnp.bfloat16)
    left_pass = jnp.einsum('rjx,cxy->rcjy', rotations.astype(jnp.float32), reference_low.astype(jnp.float32)).astype(jnp.bfloat16)
    rotated = jnp.einsum('rcjy,rly->rcjl', left_pass.astype(jnp.float32), rotations.astype(jnp.float32))
    cosine, sine_part = grid_phases(band, box)
    rot_real = rotated[:, None, 0]
    rot_imag = rotated[:, None, 1]
    shifted_real = cosine * rot_real + sine_part * rot_imag
    shifted_imag = cosine * rot_imag - sine_part * rot_real
    stacked = jnp.stack([shifted_real, shifted_imag], 2).astype(jnp.bfloat16)
    return stacked.reshape(ROT * TRANS, 2 * band * band)

def posterior(slot_rows, template_rows, band):
    scores = jnp.dot(slot_rows, template_rows.T, preferred_element_type=jnp.float32) * (2.0 / band)
    highest = lax.optimization_barrier(jnp.max(scores, 1, keepdims=True))
    exponent = jnp.exp(scores - highest)
    totals = lax.optimization_barrier(jnp.sum(exponent, 1, keepdims=True))
    weights = (exponent / totals).astype(jnp.bfloat16)
    evidence = highest[:, 0] + jnp.log(totals[:, 0]) - math.log(ROT * TRANS)
    return (weights, evidence)

def back_project(weights, slot_rows, rotations, band, box):
    gathered = jnp.dot(weights.T, slot_rows, preferred_element_type=jnp.float32)
    grid_terms = gathered.reshape(ROT, TRANS, 2, band, band)
    cosine, sine_part = grid_phases(band, box)
    grid_real = grid_terms[:, :, 0]
    grid_imag = grid_terms[:, :, 1]
    back_real = lax.optimization_barrier(jnp.sum(cosine * grid_real - sine_part * grid_imag, 1))
    back_imag = lax.optimization_barrier(jnp.sum(sine_part * grid_real + cosine * grid_imag, 1))
    direction = jnp.stack([back_real, back_imag], 1).astype(jnp.bfloat16)
    back_left = jnp.einsum('rjx,rcjl->rcxl', rotations.astype(jnp.float32), direction.astype(jnp.float32)).astype(jnp.bfloat16)
    return jnp.einsum('rcxl,rly->cxy', back_left.astype(jnp.float32), rotations.astype(jnp.float32))

def slot_ranks(flat_lists, count):
    onehot = (flat_lists[..., None] == jnp.arange(count, dtype=jnp.int32)).astype(jnp.int32)
    before = jnp.cumsum(onehot, -2) - onehot
    return lax.optimization_barrier(jnp.sum(before * onehot, -1))

def reference(particle_tiles, class_lists, offsets, defocus_groups, contrast_table, references, rotations):
    stacked = fourier_tables(BOX, BAND)
    blocks = particle_tiles.reshape(N_CLS, P_DEV, BOX, BOX)
    spectra = lax.map(lambda tile_block: band_spectra(tile_block, stacked, BAND), blocks)
    spectra = spectra.reshape(PARTICLES, 2, BAND, BAND)
    prepared = filtered(spectra, contrast_table[defocus_groups], offsets, BAND, BOX)
    flat_lists = class_lists.reshape(N_CLS, P_DEV * TOP)
    slot_rank = slot_ranks(flat_lists, K)
    position = flat_lists * CAP + slot_rank
    particle_local = jnp.arange(P_DEV * TOP, dtype=jnp.int32) // TOP

    def fill_slots(positions):
        return jnp.full((K * CAP,), -1, jnp.int32).at[positions].set(particle_local)
    source = jax.vmap(fill_slots)(position)
    device_base = (jnp.arange(N_CLS, dtype=jnp.int32) * P_DEV)[:, None]
    source = jnp.where(source >= 0, source + device_base, -1)
    slot_table = source.reshape(N_CLS, K, CAP).transpose(1, 0, 2).reshape(K, N_CLS * CAP)

    def per_class(class_item):
        entries, class_reference = class_item
        occupied = entries >= 0
        slot_rows = jnp.where(occupied[:, None, None, None], prepared[jnp.maximum(entries, 0)], 0)
        slot_rows = slot_rows.reshape(N_CLS * CAP, 2 * BAND * BAND)
        template_rows = templates(class_reference, rotations, BAND, BOX)
        weights, evidence = posterior(slot_rows, template_rows, BAND)
        numerator = back_project(weights, slot_rows, rotations, BAND, BOX)
        return (numerator, evidence)
    numerators, evidence = lax.map(per_class, (slot_table, references))
    devices = jnp.repeat(jnp.arange(N_CLS, dtype=jnp.int32), P_DEV * TOP)
    picked = evidence[flat_lists.reshape(-1), devices * CAP + slot_rank.reshape(-1)]
    return (numerators, picked.reshape(PARTICLES, TOP))
```

```python
import functools
import math

import jax
import jax.numpy as jnp
import numpy as np
from jax import lax
from jax.experimental import pallas as pl
from jax.experimental.pallas import tpu as pltpu
from jax.sharding import PartitionSpec as P

SHIFT_GRID = ((-1, -1), (-1, 0), (-1, 1), (0, -1), (0, 0), (0, 1), (1, -1), (1, 0), (1, 1))
HALF_SHIFTS = SHIFT_GRID[5:]
SHIFTS = len(SHIFT_GRID)
MIB = 1 << 20

NT = (((1,), (1,)), ((), ()))
NN = (((1,), (0,)), ((), ()))


def dot(left, right, dims):
    return lax.dot_general(left, right, dims, preferred_element_type=jnp.float32)


def signed_frequencies(band):
    counter = np.arange(band)
    return np.where(counter < band // 2, counter, counter - band)


def fourier_table(box, band):
    angles = (signed_frequencies(band)[:, None] * np.arange(box)[None, :] % box) * (2.0 * math.pi / box)
    both = np.concatenate([np.cos(angles), np.sin(angles)], 0) / math.sqrt(box)
    return both.astype(np.float32).astype(jnp.bfloat16)


def shift_tables(band, box):
    frequency = signed_frequencies(band)
    u = np.array(HALF_SHIFTS)
    residue = frequency[None, :, None] * u[:, 0, None, None] + frequency[None, None, :] * u[:, 1, None, None]
    angles = (residue % box) * (2.0 * math.pi / box)
    return np.stack([np.cos(angles), np.sin(angles)], 1).astype(np.float32)


def cos_sin(steps, box):
    quarter = box // 4
    moved = (steps + quarter // 2) & (box - 1)
    turn = moved // quarter
    angle = ((moved & (quarter - 1)) - quarter // 2).astype(jnp.float32) * (2.0 * math.pi / box)
    sq = angle * angle
    c = 1.0 + sq * (-1 / 2 + sq * (1 / 24 + sq * (-1 / 720 + sq * (1 / 40320))))
    s = angle * (1.0 + sq * (-1 / 6 + sq * (1 / 120 + sq * (-1 / 5040 + sq * (1 / 362880)))))
    odd = (turn & 1) == 1
    cosine = jnp.where(odd, s, c)
    sine = jnp.where(odd, c, s)
    cosine = jnp.where((turn == 1) | (turn == 2), -cosine, cosine)
    sine = jnp.where(turn >= 2, -sine, sine)
    return cosine, sine


def iota_frequency(shape, dim):
    band = shape[dim]
    counter = lax.broadcasted_iota(jnp.int32, shape, dim)
    return jnp.where(counter < band // 2, counter, counter - band)


def spectra_kernel(off_ref, grp_ref, tile_ref, table_ref, contrast_ref, out_ref, *, block):
    box = tile_ref.shape[-1]
    band = contrast_ref.shape[-1]
    first = pl.program_id(0) * block
    table = table_ref[...]
    lane = lax.broadcasted_iota(jnp.int32, (band, band), 1)
    row_shift = jnp.zeros((band, band), jnp.int32)
    for i in range(block):
        row_shift = jnp.where(lane == i, off_ref[first + i, 0], row_shift)
    row_cos, row_sin = cos_sin(iota_frequency((band, band), 0) * row_shift, box)
    sub = lax.broadcasted_iota(jnp.int32, (block, band), 0)
    col_shift = jnp.zeros((block, band), jnp.int32)
    for i in range(block):
        col_shift = jnp.where(sub == i, off_ref[first + i, 1], col_shift)
    col_cos, col_sin = cos_sin(iota_frequency((block, band), 1) * col_shift, box)
    for i in range(block):
        first_pass = dot(tile_ref[i], table, NT).astype(jnp.bfloat16)
        second = dot(table, first_pass, NN)
        re = (second[:band, :band] - second[band:, band:]).astype(jnp.bfloat16).astype(jnp.float32)
        im = (-(second[band:, :band] + second[:band, band:])).astype(jnp.bfloat16).astype(jnp.float32)
        rc = jnp.broadcast_to(row_cos[:, i : i + 1], (band, band))
        rs = jnp.broadcast_to(row_sin[:, i : i + 1], (band, band))
        cc, cs = col_cos[i : i + 1], col_sin[i : i + 1]
        gain = contrast_ref[grp_ref[first + i]].astype(jnp.float32)
        c = gain * (rc * cc - rs * cs)
        s = gain * (rs * cc + rc * cs)
        out_re = (c * re - s * im).astype(jnp.bfloat16).astype(jnp.float32)
        out_im = (c * im + s * re).astype(jnp.bfloat16).astype(jnp.float32)
        out_ref[0, pl.ds(i * band, band), :] = out_re
        out_ref[1, pl.ds(i * band, band), :] = out_im


def spectra(tiles, offsets, groups, table, contrast):
    count, box, _ = tiles.shape
    band = contrast.shape[-1]
    block = 8 if count % 8 == 0 else count
    return pl.pallas_call(
        functools.partial(spectra_kernel, block=block),
        grid=(count // block,),
        out_shape=jax.ShapeDtypeStruct((2, count * band, band), jnp.float32),
        in_specs=[
            pl.BlockSpec(memory_space=pltpu.SMEM),
            pl.BlockSpec(memory_space=pltpu.SMEM),
            pl.BlockSpec((block, box, box), lambda i: (i, 0, 0)),
            pl.BlockSpec(table.shape, lambda i: (0, 0)),
            pl.BlockSpec(contrast.shape, lambda i: (0, 0, 0)),
        ],
        out_specs=pl.BlockSpec((2, block * band, band), lambda i: (0, i, 0)),
        compiler_params=pltpu.CompilerParams(vmem_limit_bytes=32 * MIB),
        cost_estimate=pl.CostEstimate(
            flops=count * 4 * box**3, bytes_accessed=count * (box * box * 2 + band * band * 8), transcendentals=0
        ),
        name="spectra",
    )(offsets, groups, tiles, table, contrast)


def search_kernel(
    slot_ref, class_ref, rot_ref, rot_t_ref, phase_ref, x_ref, out_ref, ev_ref,
    work, left, shifted, score, diag, partial_sum, weight_t, *, rots, half, chunk, count, group,
):
    band = rot_ref.shape[-1]
    wide = 2 * band
    pad = shifted.shape[1]
    step_rows = 64

    @pl.when(pl.program_id(0) == 0)
    def _():
        diag[...] = jnp.zeros_like(diag)
        for r in range(rots):
            block = rot_ref[r * band : (r + 1) * band, :]
            diag[r, :band, :band] = block
            diag[r, band:, band:] = block

    for h in range(rots // half):

        @pl.loop(0, chunk)
        def _(c):
            halfway = dot(rot_ref[h * half * band : (h + 1) * half * band, :], class_ref[c], NN)
            left[0, pl.ds(c, half * band, stride=chunk), :] = halfway[:, :band]
            left[1, pl.ds(c, half * band, stride=chunk), :] = halfway[:, band:]

        @pl.loop(0, half * band // step_rows)
        def _(i):
            r = h * half + i // (band // step_rows)
            j = pl.multiple_of((i % (band // step_rows)) * step_rows, step_rows)
            at = pl.ds(pl.multiple_of(i * step_rows * chunk, 8), step_rows * chunk)
            source = jnp.concatenate([left[0, at, :], left[1, at, :]], 1).astype(jnp.bfloat16)
            turned = dot(source, diag[r], NT).astype(jnp.bfloat16)
            work[r, pl.ds(j, step_rows)] = turned.reshape(step_rows, chunk, wide)

    score[...] = jnp.zeros_like(score)

    @pl.loop(0, band // group)
    def _(g):
        ys, ts = [], []
        for k in range(group):
            j = g * group + k
            re = x_ref[0, pl.ds(j, count, stride=band), :]
            im = x_ref[1, pl.ds(j, count, stride=band), :]
            parts = [None] * SHIFTS
            parts[SHIFTS // 2] = jnp.concatenate([re, im], 1)
            for s in range(len(HALF_SHIFTS)):
                c = phase_ref[s, 0, pl.ds(j, 1), :]
                d = phase_ref[s, 1, pl.ds(j, 1), :]
                cr, ci, dr, di = c * re, c * im, d * re, d * im
                parts[SHIFTS // 2 + 1 + s] = jnp.concatenate([cr - di, dr + ci], 1)
                parts[SHIFTS // 2 - 1 - s] = jnp.concatenate([cr + di, ci - dr], 1)
            if pad > SHIFTS * count:
                parts.append(jnp.zeros((pad - SHIFTS * count, wide), jnp.float32))
            y = jnp.concatenate(parts, 0).astype(jnp.bfloat16)
            shifted[j] = y
            ys.append(y)
            ts.append(work[:, j].reshape(rots * chunk, wide))
        score[...] += dot(jnp.concatenate(ys, 1), jnp.concatenate(ts, 1), NT)

    base = pl.program_id(0) * chunk
    lane_class = lax.broadcasted_iota(jnp.int32, (count, rots * chunk), 1) & (chunk - 1)
    first = lane_class == slot_ref[:, 0:1] - base
    second = lane_class == slot_ref[:, 1:2] - base
    slabs = [score[s * count : (s + 1) * count, :] * (2.0 / band) for s in range(SHIFTS)]
    highest = functools.reduce(jnp.maximum, slabs)
    low = -3.0e38
    top0 = jnp.max(jnp.where(first, highest, low), 1, keepdims=True)
    top1 = jnp.max(jnp.where(second, highest, low), 1, keepdims=True)
    top = jnp.where(first, top0, top1)
    either = first | second
    exps = [jnp.where(either, jnp.exp(jnp.where(either, slab - top, 0.0)), 0.0) for slab in slabs]
    summed = functools.reduce(jnp.add, exps)
    total0 = jnp.sum(jnp.where(first, summed, 0.0), 1, keepdims=True)
    total1 = jnp.sum(jnp.where(second, summed, 0.0), 1, keepdims=True)
    here0 = total0 > 0.0
    here1 = total1 > 0.0
    total0 = jnp.where(here0, total0, 1.0)
    total1 = jnp.where(here1, total1, 1.0)
    total = jnp.where(first, total0, total1)
    weights = [e / total for e in exps]
    if pad > SHIFTS * count:
        weights.append(jnp.zeros((pad - SHIFTS * count, rots * chunk), jnp.float32))
    weight_t[...] = jnp.concatenate(weights, 0).T.astype(jnp.bfloat16)
    shiftless = math.log(rots * SHIFTS)
    old = jnp.where(pl.program_id(0) == 0, 0.0, ev_ref[...])
    found0 = jnp.where(here0, top0 + jnp.log(total0) - shiftless, old[:, 0:1])
    found1 = jnp.where(here1, top1 + jnp.log(total1) - shiftless, old[:, 1:2])
    ev_ref[...] = jnp.concatenate([found0, found1], 1)

    @pl.loop(0, band // group)
    def _(g):
        for k in range(group):
            j = g * group + k
            d = dot(weight_t[...], shifted[j], NN).astype(jnp.bfloat16)
            work[:, j] = d.reshape(rots, chunk, wide)

    for h in range(rots // half):

        @pl.loop(0, half * band // step_rows)
        def _(i):
            r = h * half + i // (band // step_rows)
            j = pl.multiple_of((i % (band // step_rows)) * step_rows, step_rows)
            source = work[r, pl.ds(j, step_rows)].reshape(step_rows * chunk, wide)
            turned = dot(source, diag[r], NN)
            at = pl.ds(pl.multiple_of(i * step_rows * chunk, 8), step_rows * chunk)
            left[0, at, :] = turned[:, :band]
            left[1, at, :] = turned[:, band:]

        @pl.loop(0, chunk)
        def _(c):
            at = pl.ds(c, half * band, stride=chunk)
            column = jnp.concatenate([left[0, at, :], left[1, at, :]], 1).astype(jnp.bfloat16)
            turned = dot(rot_t_ref[:, h * half * band : (h + 1) * half * band], column, NN)
            if h:
                turned += partial_sum[c]
            if h == rots // half - 1:
                out_ref[c] = turned.astype(out_ref.dtype)
            else:
                partial_sum[c] = turned


def search(slots, classes, rotations, x, box):
    n, band, wide = classes.shape
    rots = rotations.shape[0]
    count = slots.shape[0]
    chunk = min(n, 16)
    half = rots // 2 if rots % 2 == 0 else rots
    pad = -(-SHIFTS * count // 16) * 16
    rot_rows = rotations.reshape(rots * band, band)
    phases = jnp.asarray(shift_tables(band, box))
    whole = lambda shape: pl.BlockSpec(shape, lambda i: (0,) * len(shape))
    return pl.pallas_call(
        functools.partial(search_kernel, rots=rots, half=half, chunk=chunk, count=count, group=4),
        grid=(n // chunk,),
        out_shape=[
            jax.ShapeDtypeStruct((n, band, wide), jnp.bfloat16),
            jax.ShapeDtypeStruct((count, 2), jnp.float32),
        ],
        in_specs=[
            whole((count, 2)),
            pl.BlockSpec((chunk, band, wide), lambda i: (i, 0, 0)),
            whole((rots * band, band)),
            whole((band, rots * band)),
            whole(phases.shape),
            whole(x.shape),
        ],
        out_specs=[pl.BlockSpec((chunk, band, wide), lambda i: (i, 0, 0)), whole((count, 2))],
        scratch_shapes=[
            pltpu.VMEM((rots, band, chunk, wide), jnp.bfloat16),
            pltpu.VMEM((2, half * band * chunk, band), jnp.float32),
            pltpu.VMEM((band, pad, wide), jnp.bfloat16),
            pltpu.VMEM((pad, rots * chunk), jnp.float32),
            pltpu.VMEM((rots, wide, wide), jnp.bfloat16),
            pltpu.VMEM((chunk, band, wide), jnp.float32),
            pltpu.VMEM((rots * chunk, pad), jnp.bfloat16),
        ],
        compiler_params=pltpu.CompilerParams(vmem_limit_bytes=62 * MIB),
        cost_estimate=pl.CostEstimate(flops=10**10, bytes_accessed=10**7, transcendentals=0),
        name="search",
    )(slots, classes, rot_rows, rot_rows.T, phases, x)


def bit_order(n):
    bits = n.bit_length() - 1
    return list(range(bits - 1, -1, -1))


def swap(value, axis, bit, n):
    return lax.ppermute(value, axis, [(i, i ^ (1 << bit)) for i in range(n)])


def on_device(tiles, class_lists, offsets, defocus_groups, contrast_table, references, rotations):
    n = lax.axis_size("cls")
    me = lax.axis_index("cls")
    box = tiles.shape[-1]
    band = references.shape[-1]
    order = bit_order(n)

    classes = references.astype(jnp.bfloat16).transpose(0, 2, 1, 3).reshape(1, band, 2 * band)
    for bit in order:
        classes = jnp.concatenate([classes, swap(classes, "cls", bit, n)], 0)

    relative = class_lists ^ me
    slots = functools.reduce(jnp.add, [((relative >> bit) & 1) << t for t, bit in enumerate(order)])

    x = spectra(tiles, offsets, defocus_groups, jnp.asarray(fourier_table(box, band)), contrast_table)
    sums, evidence = search(slots, classes, rotations, x, box)

    for bit in reversed(order):
        keep, give = jnp.split(sums, 2, 0)
        got = swap(give, "cls", bit, n)
        sums = keep.astype(jnp.float32) + got.astype(jnp.float32)
        if bit != order[0]:
            sums = sums.astype(jnp.bfloat16)
    numerators = sums.reshape(1, band, 2, band).transpose(0, 2, 1, 3)
    return numerators, evidence


def solution(mesh):
    return jax.shard_map(
        on_device,
        mesh=mesh,
        in_specs=(
            P(("groups", "cls"), None, None),
            P(("groups", "cls"), None),
            P(("groups", "cls"), None),
            P(("groups", "cls")),
            P(),
            P(("groups", "cls"), None, None, None),
            P(),
        ),
        out_specs=(P(("groups", "cls"), None, None, None), P(("groups", "cls"), None)),
        check_vma=False,
    )
```

```python
import functools
import math

import jax
import jax.numpy as jnp
import numpy as np
from jax import lax
from jax.experimental import pallas as pl
from jax.experimental.pallas import tpu as pltpu
from jax.sharding import PartitionSpec as P

SHIFT_GRID = ((-1, -1), (-1, 0), (-1, 1), (0, -1), (0, 0), (0, 1), (1, -1), (1, 0), (1, 1))
HALF_SHIFTS = SHIFT_GRID[5:]
SHIFTS = len(SHIFT_GRID)
MIB = 1 << 20

NT = (((1,), (1,)), ((), ()))
NN = (((1,), (0,)), ((), ()))


def dot(left, right, dims):
    return lax.dot_general(left, right, dims, preferred_element_type=jnp.float32)


def signed_frequencies(band):
    counter = np.arange(band)
    return np.where(counter < band // 2, counter, counter - band)


def fourier_table(box, band):
    angles = (signed_frequencies(band)[:, None] * np.arange(box)[None, :] % box) * (2.0 * math.pi / box)
    both = np.concatenate([np.cos(angles), np.sin(angles)], 0) / math.sqrt(box)
    return both.astype(np.float32).astype(jnp.bfloat16)


def shift_tables(band, box):
    frequency = signed_frequencies(band)
    u = np.array(HALF_SHIFTS)
    residue = frequency[None, :, None] * u[:, 0, None, None] + frequency[None, None, :] * u[:, 1, None, None]
    angles = (residue % box) * (2.0 * math.pi / box)
    return np.stack([np.cos(angles), np.sin(angles)], 1).astype(np.float32)


def cos_sin(steps, box):
    quarter = box // 4
    moved = (steps + quarter // 2) & (box - 1)
    turn = moved // quarter
    angle = ((moved & (quarter - 1)) - quarter // 2).astype(jnp.float32) * (2.0 * math.pi / box)
    sq = angle * angle
    c = 1.0 + sq * (-1 / 2 + sq * (1 / 24 + sq * (-1 / 720 + sq * (1 / 40320))))
    s = angle * (1.0 + sq * (-1 / 6 + sq * (1 / 120 + sq * (-1 / 5040 + sq * (1 / 362880)))))
    odd = (turn & 1) == 1
    cosine = jnp.where(odd, s, c)
    sine = jnp.where(odd, c, s)
    cosine = jnp.where((turn == 1) | (turn == 2), -cosine, cosine)
    sine = jnp.where(turn >= 2, -sine, sine)
    return cosine, sine


def iota_frequency(shape, dim):
    band = shape[dim]
    counter = lax.broadcasted_iota(jnp.int32, shape, dim)
    return jnp.where(counter < band // 2, counter, counter - band)


def spectra_kernel(off_ref, grp_ref, tile_ref, table_ref, contrast_ref, out_ref, *, block):
    box = tile_ref.shape[-1]
    band = contrast_ref.shape[-1]
    first = pl.program_id(0) * block
    table = table_ref[...]
    lane = lax.broadcasted_iota(jnp.int32, (band, band), 1)
    row_shift = jnp.zeros((band, band), jnp.int32)
    for i in range(block):
        row_shift = jnp.where(lane == i, off_ref[first + i, 0], row_shift)
    row_cos, row_sin = cos_sin(iota_frequency((band, band), 0) * row_shift, box)
    sub = lax.broadcasted_iota(jnp.int32, (block, band), 0)
    col_shift = jnp.zeros((block, band), jnp.int32)
    for i in range(block):
        col_shift = jnp.where(sub == i, off_ref[first + i, 1], col_shift)
    col_cos, col_sin = cos_sin(iota_frequency((block, band), 1) * col_shift, box)
    for i in range(block):
        first_pass = dot(tile_ref[i], table, NT).astype(jnp.bfloat16)
        second = dot(table, first_pass, NN)
        re = (second[:band, :band] - second[band:, band:]).astype(jnp.bfloat16).astype(jnp.float32)
        im = (-(second[band:, :band] + second[:band, band:])).astype(jnp.bfloat16).astype(jnp.float32)
        rc = jnp.broadcast_to(row_cos[:, i : i + 1], (band, band))
        rs = jnp.broadcast_to(row_sin[:, i : i + 1], (band, band))
        cc, cs = col_cos[i : i + 1], col_sin[i : i + 1]
        gain = contrast_ref[grp_ref[first + i]].astype(jnp.float32)
        c = gain * (rc * cc - rs * cs)
        s = gain * (rs * cc + rc * cs)
        out_re = (c * re - s * im).astype(jnp.bfloat16).astype(jnp.float32)
        out_im = (c * im + s * re).astype(jnp.bfloat16).astype(jnp.float32)
        out_ref[0, 0, pl.ds(i, band, stride=block), :] = out_re
        out_ref[0, 1, pl.ds(i, band, stride=block), :] = out_im


def spectra(tiles, offsets, groups, table, contrast):
    count, box, _ = tiles.shape
    band = contrast.shape[-1]
    block = 8 if count % 8 == 0 else count
    return pl.pallas_call(
        functools.partial(spectra_kernel, block=block),
        grid=(count // block,),
        out_shape=jax.ShapeDtypeStruct((count // block, 2, band * block, band), jnp.float32),
        in_specs=[
            pl.BlockSpec(memory_space=pltpu.SMEM),
            pl.BlockSpec(memory_space=pltpu.SMEM),
            pl.BlockSpec((block, box, box), lambda i: (i, 0, 0)),
            pl.BlockSpec(table.shape, lambda i: (0, 0)),
            pl.BlockSpec(contrast.shape, lambda i: (0, 0, 0)),
        ],
        out_specs=pl.BlockSpec((1, 2, band * block, band), lambda i: (i, 0, 0, 0)),
        compiler_params=pltpu.CompilerParams(vmem_limit_bytes=32 * MIB),
        cost_estimate=pl.CostEstimate(
            flops=count * 4 * box**3, bytes_accessed=count * (box * box * 2 + band * band * 8), transcendentals=0
        ),
        name="spectra",
    )(offsets, groups, tiles, table, contrast)


def search_kernel(
    slot_ref, class_ref, rot_ref, rot_t_ref, phase_ref, x_ref, out_ref, ev_ref,
    work, left, shifted, score, diag, partial_sum, weight_t, *, rots, half, chunk, count, group,
):
    band = rot_ref.shape[-1]
    wide = 2 * band
    pad = shifted.shape[1]
    block = x_ref.shape[2] // band
    eights = chunk // 8
    classes_step = 4
    rots_step = 2 if half % 2 == 0 else 1

    @pl.when(pl.program_id(0) == 0)
    def _():
        diag[...] = jnp.zeros_like(diag)
        for r in range(rots):
            block = rot_ref[r * band : (r + 1) * band, :]
            diag[r, :band, :band] = block
            diag[r, band:, band:] = block

    for h in range(rots // half):

        @pl.loop(0, chunk // classes_step)
        def _(g):
            for k in range(classes_step):
                c = g * classes_step + k
                halfway = dot(rot_ref[h * half * band : (h + 1) * half * band, :], class_ref[c], NN)
                at = pl.ds(c % 8, half * band, stride=8)
                left[0, c // 8, at, :] = halfway[:, :band]
                left[1, c // 8, at, :] = halfway[:, band:]

        @pl.loop(0, half // rots_step)
        def _(g):
            for k in range(rots_step):
                r = g * rots_step + k
                at = pl.ds(pl.multiple_of(r * band * 8, 8), band * 8)
                parts = [
                    jnp.concatenate([left[q, e, at, :].reshape(band, 8, band) for e in range(eights)], 1)
                    for q in range(2)
                ]
                source = jnp.concatenate(parts, 2).reshape(band * chunk, wide).astype(jnp.bfloat16)
                turned = dot(source, diag[h * half + r], NT).astype(jnp.bfloat16)
                work[h * half + r] = turned.reshape(band, chunk, wide)

    score[...] = jnp.zeros_like(score)

    @pl.loop(0, band // group)
    def _(g):
        ys, ts = [], []
        for k in range(group):
            j = g * group + k
            at = pl.ds(pl.multiple_of(j * block, 8), block)
            re = jnp.concatenate([x_ref[b, 0, at, :] for b in range(count // block)], 0)
            im = jnp.concatenate([x_ref[b, 1, at, :] for b in range(count // block)], 0)
            parts = [None] * SHIFTS
            parts[SHIFTS // 2] = jnp.concatenate([re, im], 1)
            for s in range(len(HALF_SHIFTS)):
                c = phase_ref[s, 0, pl.ds(j, 1), :]
                d = phase_ref[s, 1, pl.ds(j, 1), :]
                cr, ci, dr, di = c * re, c * im, d * re, d * im
                parts[SHIFTS // 2 + 1 + s] = jnp.concatenate([cr - di, dr + ci], 1)
                parts[SHIFTS // 2 - 1 - s] = jnp.concatenate([cr + di, ci - dr], 1)
            if pad > SHIFTS * count:
                parts.append(jnp.zeros((pad - SHIFTS * count, wide), jnp.float32))
            y = jnp.concatenate(parts, 0).astype(jnp.bfloat16)
            shifted[j] = y
            ys.append(y)
            ts.append(work[:, j].reshape(rots * chunk, wide))
        score[...] += dot(jnp.concatenate(ys, 1), jnp.concatenate(ts, 1), NT)

    base = pl.program_id(0) * chunk
    lane_class = lax.broadcasted_iota(jnp.int32, (count, rots * chunk), 1) & (chunk - 1)
    first = lane_class == slot_ref[:, 0:1] - base
    second = lane_class == slot_ref[:, 1:2] - base
    slabs = [score[s * count : (s + 1) * count, :] * (2.0 / band) for s in range(SHIFTS)]
    highest = functools.reduce(jnp.maximum, slabs)
    low = -3.0e38
    top0 = jnp.max(jnp.where(first, highest, low), 1, keepdims=True)
    top1 = jnp.max(jnp.where(second, highest, low), 1, keepdims=True)
    top = jnp.where(first, top0, top1)
    either = first | second
    exps = [jnp.where(either, jnp.exp(jnp.where(either, slab - top, 0.0)), 0.0) for slab in slabs]
    summed = functools.reduce(jnp.add, exps)
    total0 = jnp.sum(jnp.where(first, summed, 0.0), 1, keepdims=True)
    total1 = jnp.sum(jnp.where(second, summed, 0.0), 1, keepdims=True)
    here0 = total0 > 0.0
    here1 = total1 > 0.0
    total0 = jnp.where(here0, total0, 1.0)
    total1 = jnp.where(here1, total1, 1.0)
    total = jnp.where(first, total0, total1)
    weights = [e / total for e in exps]
    if pad > SHIFTS * count:
        weights.append(jnp.zeros((pad - SHIFTS * count, rots * chunk), jnp.float32))
    weight_t[...] = jnp.concatenate(weights, 0).T.astype(jnp.bfloat16)
    shiftless = math.log(rots * SHIFTS)
    old = jnp.where(pl.program_id(0) == 0, 0.0, ev_ref[...])
    found0 = jnp.where(here0, top0 + jnp.log(total0) - shiftless, old[:, 0:1])
    found1 = jnp.where(here1, top1 + jnp.log(total1) - shiftless, old[:, 1:2])
    ev_ref[...] = jnp.concatenate([found0, found1], 1)

    @pl.loop(0, band // group)
    def _(g):
        for k in range(group):
            j = g * group + k
            d = dot(weight_t[...], shifted[j], NN).astype(jnp.bfloat16)
            work[:, j] = d.reshape(rots, chunk, wide)

    for h in range(rots // half):

        @pl.loop(0, half // rots_step)
        def _(g):
            for k in range(rots_step):
                r = g * rots_step + k
                turned = dot(work[h * half + r].reshape(band * chunk, wide), diag[h * half + r], NN)
                turned = turned.reshape(band, chunk, wide)
                at = pl.ds(pl.multiple_of(r * band * 8, 8), band * 8)
                for q in range(2):
                    for e in range(eights):
                        piece = turned[:, e * 8 : (e + 1) * 8, q * band : (q + 1) * band]
                        left[q, e, at, :] = piece.reshape(band * 8, band)

        @pl.loop(0, chunk // classes_step)
        def _(g):
            for k in range(classes_step):
                c = g * classes_step + k
                at = pl.ds(c % 8, half * band, stride=8)
                column = jnp.concatenate([left[0, c // 8, at, :], left[1, c // 8, at, :]], 1).astype(jnp.bfloat16)
                turned = dot(rot_t_ref[:, h * half * band : (h + 1) * half * band], column, NN)
                if h:
                    turned += partial_sum[c]
                if h == rots // half - 1:
                    out_ref[c] = turned.astype(out_ref.dtype)
                else:
                    partial_sum[c] = turned


def search(slots, classes, rotations, x, box):
    n, band, wide = classes.shape
    rots = rotations.shape[0]
    count = slots.shape[0]
    chunk = min(n, 16)
    half = rots // 2 if rots % 2 == 0 else rots
    pad = -(-SHIFTS * count // 16) * 16
    rot_rows = rotations.reshape(rots * band, band)
    phases = jnp.asarray(shift_tables(band, box))
    whole = lambda shape: pl.BlockSpec(shape, lambda i: (0,) * len(shape))
    return pl.pallas_call(
        functools.partial(search_kernel, rots=rots, half=half, chunk=chunk, count=count, group=16),
        grid=(n // chunk,),
        out_shape=[
            jax.ShapeDtypeStruct((n, band, wide), jnp.bfloat16),
            jax.ShapeDtypeStruct((count, 2), jnp.float32),
        ],
        in_specs=[
            whole((count, 2)),
            pl.BlockSpec((chunk, band, wide), lambda i: (i, 0, 0)),
            whole((rots * band, band)),
            whole((band, rots * band)),
            whole(phases.shape),
            whole(x.shape),
        ],
        out_specs=[pl.BlockSpec((chunk, band, wide), lambda i: (i, 0, 0)), whole((count, 2))],
        scratch_shapes=[
            pltpu.VMEM((rots, band, chunk, wide), jnp.bfloat16),
            pltpu.VMEM((2, chunk // 8, half * band * 8, band), jnp.float32),
            pltpu.VMEM((band, pad, wide), jnp.bfloat16),
            pltpu.VMEM((pad, rots * chunk), jnp.float32),
            pltpu.VMEM((rots, wide, wide), jnp.bfloat16),
            pltpu.VMEM((chunk, band, wide), jnp.float32),
            pltpu.VMEM((rots * chunk, pad), jnp.bfloat16),
        ],
        compiler_params=pltpu.CompilerParams(vmem_limit_bytes=62 * MIB),
        cost_estimate=pl.CostEstimate(flops=10**10, bytes_accessed=10**7, transcendentals=0),
        name="search",
    )(slots, classes, rot_rows, rot_rows.T, phases, x)


def bit_order(n):
    bits = n.bit_length() - 1
    return list(range(bits - 1, -1, -1))


def swap(value, axis, bit, n):
    return lax.ppermute(value, axis, [(i, i ^ (1 << bit)) for i in range(n)])


def on_device(tiles, class_lists, offsets, defocus_groups, contrast_table, references, rotations):
    n = lax.axis_size("cls")
    me = lax.axis_index("cls")
    box = tiles.shape[-1]
    band = references.shape[-1]
    order = bit_order(n)

    classes = references.astype(jnp.bfloat16).transpose(0, 2, 1, 3).reshape(1, band, 2 * band)
    for bit in order:
        classes = jnp.concatenate([classes, swap(classes, "cls", bit, n)], 0)

    relative = class_lists ^ me
    slots = functools.reduce(jnp.add, [((relative >> bit) & 1) << t for t, bit in enumerate(order)])

    x = spectra(tiles, offsets, defocus_groups, jnp.asarray(fourier_table(box, band)), contrast_table)
    sums, evidence = search(slots, classes, rotations, x, box)

    for bit in reversed(order):
        keep, give = jnp.split(sums, 2, 0)
        got = swap(give, "cls", bit, n)
        sums = keep.astype(jnp.float32) + got.astype(jnp.float32)
        if bit != order[0]:
            sums = sums.astype(jnp.bfloat16)
    numerators = sums.reshape(1, band, 2, band).transpose(0, 2, 1, 3)
    return numerators, evidence


def solution(mesh):
    return jax.shard_map(
        on_device,
        mesh=mesh,
        in_specs=(
            P(("groups", "cls"), None, None),
            P(("groups", "cls"), None),
            P(("groups", "cls"), None),
            P(("groups", "cls")),
            P(),
            P(("groups", "cls"), None, None, None),
            P(),
        ),
        out_specs=(P(("groups", "cls"), None, None, None), P(("groups", "cls"), None)),
        check_vma=False,
    )
```

```python
import functools
import math

import jax
import jax.numpy as jnp
import numpy as np
from jax import lax
from jax.experimental import pallas as pl
from jax.experimental.pallas import tpu as pltpu
from jax.sharding import PartitionSpec as P

SHIFT_GRID = ((-1, -1), (-1, 0), (-1, 1), (0, -1), (0, 0), (0, 1), (1, -1), (1, 0), (1, 1))
HALF_SHIFTS = SHIFT_GRID[5:]
SHIFTS = len(SHIFT_GRID)
MIB = 1 << 20

NT = (((1,), (1,)), ((), ()))
NN = (((1,), (0,)), ((), ()))


def dot(left, right, dims):
    return lax.dot_general(left, right, dims, preferred_element_type=jnp.float32)


def signed_frequencies(band):
    counter = np.arange(band)
    return np.where(counter < band // 2, counter, counter - band)


def fourier_table(box, band):
    angles = (signed_frequencies(band)[:, None] * np.arange(box)[None, :] % box) * (2.0 * math.pi / box)
    both = np.concatenate([np.cos(angles), np.sin(angles)], 0) / math.sqrt(box)
    return both.astype(np.float32).astype(jnp.bfloat16)


def shift_tables(band, box):
    frequency = signed_frequencies(band)
    u = np.array(HALF_SHIFTS)
    residue = frequency[None, :, None] * u[:, 0, None, None] + frequency[None, None, :] * u[:, 1, None, None]
    angles = (residue % box) * (2.0 * math.pi / box)
    return np.stack([np.cos(angles), np.sin(angles)], 1).astype(np.float32)


def cos_sin(steps, box):
    quarter = box // 4
    moved = (steps + quarter // 2) & (box - 1)
    turn = moved // quarter
    angle = ((moved & (quarter - 1)) - quarter // 2).astype(jnp.float32) * (2.0 * math.pi / box)
    sq = angle * angle
    c = 1.0 + sq * (-1 / 2 + sq * (1 / 24 + sq * (-1 / 720 + sq * (1 / 40320))))
    s = angle * (1.0 + sq * (-1 / 6 + sq * (1 / 120 + sq * (-1 / 5040 + sq * (1 / 362880)))))
    odd = (turn & 1) == 1
    cosine = jnp.where(odd, s, c)
    sine = jnp.where(odd, c, s)
    cosine = jnp.where((turn == 1) | (turn == 2), -cosine, cosine)
    sine = jnp.where(turn >= 2, -sine, sine)
    return cosine, sine


def iota_frequency(shape, dim):
    band = shape[dim]
    counter = lax.broadcasted_iota(jnp.int32, shape, dim)
    return jnp.where(counter < band // 2, counter, counter - band)


def spectra_kernel(grp_ref, off_ref, tile_ref, table_ref, contrast_ref, out_ref, *, block):
    box = tile_ref.shape[-1]
    band = contrast_ref.shape[-1]
    first = pl.program_id(0) * block
    table = table_ref[...]
    moved = off_ref[pl.ds(pl.multiple_of(first, block), block), :]
    row_shift = jnp.broadcast_to(moved[:, 0:1], (block, band))
    lane = lax.broadcasted_iota(jnp.int32, (block, band), 1)
    sub = lax.broadcasted_iota(jnp.int32, (block, band), 0)
    row_shift = jnp.sum(jnp.where(lane == sub, row_shift, 0), 0, keepdims=True)
    row_cos, row_sin = cos_sin(iota_frequency((band, band), 0) * row_shift, box)
    col_cos, col_sin = cos_sin(iota_frequency((block, band), 1) * moved[:, 1:2], box)
    for i in range(block):
        first_pass = dot(tile_ref[i], table, NT).astype(jnp.bfloat16)
        second = dot(table, first_pass, NN)
        re = (second[:band, :band] - second[band:, band:]).astype(jnp.bfloat16).astype(jnp.float32)
        im = (-(second[band:, :band] + second[:band, band:])).astype(jnp.bfloat16).astype(jnp.float32)
        rc = jnp.broadcast_to(row_cos[:, i : i + 1], (band, band))
        rs = jnp.broadcast_to(row_sin[:, i : i + 1], (band, band))
        cc, cs = col_cos[i : i + 1], col_sin[i : i + 1]
        gain = contrast_ref[grp_ref[first + i]].astype(jnp.float32)
        c = gain * (rc * cc - rs * cs)
        s = gain * (rs * cc + rc * cs)
        out_re = (c * re - s * im).astype(jnp.bfloat16).astype(jnp.float32)
        out_im = (c * im + s * re).astype(jnp.bfloat16).astype(jnp.float32)
        out_ref[0, 0, pl.ds(i, band, stride=block), :] = out_re
        out_ref[0, 1, pl.ds(i, band, stride=block), :] = out_im


def spectra(tiles, offsets, groups, table, contrast):
    count, box, _ = tiles.shape
    band = contrast.shape[-1]
    block = 8 if count % 8 == 0 else count
    return pl.pallas_call(
        functools.partial(spectra_kernel, block=block),
        grid=(count // block,),
        out_shape=jax.ShapeDtypeStruct((count // block, 2, band * block, band), jnp.float32),
        in_specs=[
            pl.BlockSpec(memory_space=pltpu.SMEM),
            pl.BlockSpec(offsets.shape, lambda i: (0, 0)),
            pl.BlockSpec((block, box, box), lambda i: (i, 0, 0)),
            pl.BlockSpec(table.shape, lambda i: (0, 0)),
            pl.BlockSpec(contrast.shape, lambda i: (0, 0, 0)),
        ],
        out_specs=pl.BlockSpec((1, 2, band * block, band), lambda i: (i, 0, 0, 0)),
        compiler_params=pltpu.CompilerParams(vmem_limit_bytes=32 * MIB),
        cost_estimate=pl.CostEstimate(
            flops=count * 4 * box**3, bytes_accessed=count * (box * box * 2 + band * band * 8), transcendentals=0
        ),
        name="spectra",
    )(groups, offsets, tiles, table, contrast)


def search_kernel(
    me_ref, list_ref, class_ref, rot_ref, phase_ref, x_ref, *refs, rots, half, chunk, count, group, order,
):
    *out_refs, ev_ref, work, left, shifted, score, diag, rot_t, partial_sum, weight_t = refs
    band = rot_ref.shape[-1]
    wide = 2 * band
    pad = shifted.shape[1]
    block = x_ref.shape[2] // band
    eights = chunk // 8
    classes_step = 4
    rots_step = 2 if half % 2 == 0 else 1

    @pl.when(pl.program_id(0) == 0)
    def _():
        diag[...] = jnp.zeros_like(diag)
        for r in range(rots):
            block = rot_ref[r * band : (r + 1) * band, :]
            diag[r, :band, :band] = block
            diag[r, band:, band:] = block
            rot_t[:, r * band : (r + 1) * band] = block.astype(jnp.float32).T.astype(jnp.bfloat16)

    for h in range(rots // half):

        @pl.loop(0, chunk // classes_step)
        def _(g):
            for k in range(classes_step):
                c = g * classes_step + k
                both = jnp.concatenate([class_ref[c, 0], class_ref[c, 1]], 1)
                halfway = dot(rot_ref[h * half * band : (h + 1) * half * band, :], both, NN)
                at = pl.ds(c % 8, half * band, stride=8)
                left[0, c // 8, at, :] = halfway[:, :band]
                left[1, c // 8, at, :] = halfway[:, band:]

        @pl.loop(0, half // rots_step)
        def _(g):
            for k in range(rots_step):
                r = g * rots_step + k
                at = pl.ds(pl.multiple_of(r * band * 8, 8), band * 8)
                parts = [
                    jnp.concatenate([left[q, e, at, :].reshape(band, 8, band) for e in range(eights)], 1)
                    for q in range(2)
                ]
                source = jnp.concatenate(parts, 2).reshape(band * chunk, wide).astype(jnp.bfloat16)
                turned = dot(source, diag[h * half + r], NT).astype(jnp.bfloat16)
                work[h * half + r] = turned.reshape(band, chunk, wide)

    score[...] = jnp.zeros_like(score)

    @pl.loop(0, band // group)
    def _(g):
        ys, ts = [], []
        for k in range(group):
            j = g * group + k
            at = pl.ds(pl.multiple_of(j * block, 8), block)
            re = jnp.concatenate([x_ref[b, 0, at, :] for b in range(count // block)], 0)
            im = jnp.concatenate([x_ref[b, 1, at, :] for b in range(count // block)], 0)
            parts = [None] * SHIFTS
            parts[SHIFTS // 2] = jnp.concatenate([re, im], 1)
            for s in range(len(HALF_SHIFTS)):
                c = phase_ref[s, 0, pl.ds(j, 1), :]
                d = phase_ref[s, 1, pl.ds(j, 1), :]
                cr, ci, dr, di = c * re, c * im, d * re, d * im
                parts[SHIFTS // 2 + 1 + s] = jnp.concatenate([cr - di, dr + ci], 1)
                parts[SHIFTS // 2 - 1 - s] = jnp.concatenate([cr + di, ci - dr], 1)
            if pad > SHIFTS * count:
                parts.append(jnp.zeros((pad - SHIFTS * count, wide), jnp.float32))
            y = jnp.concatenate(parts, 0).astype(jnp.bfloat16)
            shifted[j] = y
            ys.append(y)
            ts.append(work[:, j].reshape(rots * chunk, wide))
        score[...] += dot(jnp.concatenate(ys, 1), jnp.concatenate(ts, 1), NT)

    base = pl.program_id(0) * chunk
    lane_class = lax.broadcasted_iota(jnp.int32, (count, rots * chunk), 1) & (chunk - 1)
    relative = list_ref[...] ^ me_ref[0]
    slots = functools.reduce(jnp.add, [((relative >> bit) & 1) << t for t, bit in enumerate(order)])
    first = lane_class == slots[:, 0:1] - base
    second = lane_class == slots[:, 1:2] - base
    slabs = [score[s * count : (s + 1) * count, :] * (2.0 / band) for s in range(SHIFTS)]
    highest = functools.reduce(jnp.maximum, slabs)
    low = -3.0e38
    top0 = jnp.max(jnp.where(first, highest, low), 1, keepdims=True)
    top1 = jnp.max(jnp.where(second, highest, low), 1, keepdims=True)
    top = jnp.where(first, top0, top1)
    either = first | second
    exps = [jnp.where(either, jnp.exp(jnp.where(either, slab - top, 0.0)), 0.0) for slab in slabs]
    summed = functools.reduce(jnp.add, exps)
    total0 = jnp.sum(jnp.where(first, summed, 0.0), 1, keepdims=True)
    total1 = jnp.sum(jnp.where(second, summed, 0.0), 1, keepdims=True)
    here0 = total0 > 0.0
    here1 = total1 > 0.0
    total0 = jnp.where(here0, total0, 1.0)
    total1 = jnp.where(here1, total1, 1.0)
    total = jnp.where(first, total0, total1)
    weights = [e / total for e in exps]
    if pad > SHIFTS * count:
        weights.append(jnp.zeros((pad - SHIFTS * count, rots * chunk), jnp.float32))
    weight_t[...] = jnp.concatenate(weights, 0).T.astype(jnp.bfloat16)
    shiftless = math.log(rots * SHIFTS)
    old = jnp.where(pl.program_id(0) == 0, 0.0, ev_ref[...])
    found0 = jnp.where(here0, top0 + jnp.log(total0) - shiftless, old[:, 0:1])
    found1 = jnp.where(here1, top1 + jnp.log(total1) - shiftless, old[:, 1:2])
    ev_ref[...] = jnp.concatenate([found0, found1], 1)

    @pl.loop(0, band // group)
    def _(g):
        for k in range(group):
            j = g * group + k
            d = dot(weight_t[...], shifted[j], NN).astype(jnp.bfloat16)
            work[:, j] = d.reshape(rots, chunk, wide)

    for h in range(rots // half):

        @pl.loop(0, half // rots_step)
        def _(g):
            for k in range(rots_step):
                r = g * rots_step + k
                turned = dot(work[h * half + r].reshape(band * chunk, wide), diag[h * half + r], NN)
                turned = turned.reshape(band, chunk, wide)
                at = pl.ds(pl.multiple_of(r * band * 8, 8), band * 8)
                for q in range(2):
                    for e in range(eights):
                        piece = turned[:, e * 8 : (e + 1) * 8, q * band : (q + 1) * band]
                        left[q, e, at, :] = piece.reshape(band * 8, band)

        for e in range(eights):

            @pl.loop(0, 8 // classes_step)
            def _(g):
                for k in range(classes_step):
                    c = g * classes_step + k
                    at = pl.ds(c, half * band, stride=8)
                    column = jnp.concatenate([left[0, e, at, :], left[1, e, at, :]], 1).astype(jnp.bfloat16)
                    turned = dot(rot_t[:, h * half * band : (h + 1) * half * band], column, NN)
                    if h:
                        turned += partial_sum[e * 8 + c]
                    if h < rots // half - 1:
                        partial_sum[e * 8 + c] = turned
                    elif len(out_refs) == 1:
                        out_refs[0][e * 8 + c, 0] = turned[:, :band].astype(jnp.bfloat16)
                        out_refs[0][e * 8 + c, 1] = turned[:, band:].astype(jnp.bfloat16)
                    else:
                        out_refs[e][c, 0] = turned[:, :band].astype(jnp.bfloat16)
                        out_refs[e][c, 1] = turned[:, band:].astype(jnp.bfloat16)


def search(me, lists, classes, rotations, x, box, order):
    n, _, band, _ = classes.shape
    wide = 2 * band
    rots = rotations.shape[0]
    count = lists.shape[0]
    chunk = min(n, 16)
    half = rots // 2 if rots % 2 == 0 else rots
    pad = -(-SHIFTS * count // 16) * 16
    phases = jnp.asarray(shift_tables(band, box))
    whole = lambda shape: pl.BlockSpec(shape, lambda i: (0,) * len(shape))
    outs = 2 if n == chunk == 16 else 1
    out_block = (chunk // outs, 2, band, band)
    *sums, evidence = pl.pallas_call(
        functools.partial(
            search_kernel, rots=rots, half=half, chunk=chunk, count=count, group=16, order=order
        ),
        grid=(n // chunk,),
        out_shape=[jax.ShapeDtypeStruct((n // outs, 2, band, band), jnp.bfloat16)] * outs
        + [jax.ShapeDtypeStruct((count, 2), jnp.float32)],
        in_specs=[
            pl.BlockSpec(memory_space=pltpu.SMEM),
            whole((count, 2)),
            pl.BlockSpec((chunk, 2, band, band), lambda i: (i, 0, 0, 0)),
            whole((rots * band, band)),
            whole(phases.shape),
            whole(x.shape),
        ],
        out_specs=[pl.BlockSpec(out_block, lambda i: (i, 0, 0, 0))] * outs + [whole((count, 2))],
        scratch_shapes=[
            pltpu.VMEM((rots, band, chunk, wide), jnp.bfloat16),
            pltpu.VMEM((2, chunk // 8, half * band * 8, band), jnp.float32),
            pltpu.VMEM((band, pad, wide), jnp.bfloat16),
            pltpu.VMEM((pad, rots * chunk), jnp.float32),
            pltpu.VMEM((rots, wide, wide), jnp.bfloat16),
            pltpu.VMEM((band, rots * band), jnp.bfloat16),
            pltpu.VMEM((chunk, band, wide), jnp.float32),
            pltpu.VMEM((rots * chunk, pad), jnp.bfloat16),
        ],
        compiler_params=pltpu.CompilerParams(vmem_limit_bytes=62 * MIB),
        cost_estimate=pl.CostEstimate(flops=10**10, bytes_accessed=10**7, transcendentals=0),
        name="search",
    )(me, lists, classes, rotations.reshape(rots * band, band), phases, x)
    return sums if outs == 2 else jnp.split(sums[0], 2, 0), evidence


def rounds(n):
    bits = list(range(n.bit_length() - 2, 0, -1))
    return [tuple(bits[i : i + 2]) for i in range(0, len(bits), 2)] + [(0,)]


def masks(bits):
    count = len(bits)
    return [sum(((i >> t) & 1) << bits[count - 1 - t] for t in range(count)) for i in range(1, 1 << count)]


def swap(value, mask, n):
    return lax.ppermute(value, "cls", [(i, i ^ mask) for i in range(n)])


def on_device(tiles, class_lists, offsets, defocus_groups, contrast_table, references, rotations):
    n = lax.axis_size("cls")
    me = jnp.full((1,), lax.axis_index("cls"), jnp.int32)
    box = tiles.shape[-1]
    band = references.shape[-1]
    plan = rounds(n)
    order = [bit for bits in plan for bit in reversed(bits)]

    x = spectra(tiles, offsets, defocus_groups, jnp.asarray(fourier_table(box, band)), contrast_table)
    classes = references.astype(jnp.bfloat16)
    for step, bits in enumerate(plan):
        classes = jnp.concatenate([classes] + [swap(classes, mask, n) for mask in masks(bits)], 0)
        if step == 0:
            classes, x = lax.optimization_barrier((classes, x))

    (keep, give), evidence = search(me, class_lists, classes, rotations, x, box, order)

    sums = keep.astype(jnp.float32) + swap(give, 1, n).astype(jnp.float32)
    for bits in reversed(plan[:-1]):
        parts = jnp.split(sums.astype(jnp.bfloat16), 1 << len(bits), 0)
        got = [swap(part, mask, n) for part, mask in zip(parts[1:], masks(bits))]
        sums = functools.reduce(jnp.add, [part.astype(jnp.float32) for part in parts[:1] + got])
    return sums, evidence


def solution(mesh):
    return jax.shard_map(
        on_device,
        mesh=mesh,
        in_specs=(
            P(("groups", "cls"), None, None),
            P(("groups", "cls"), None),
            P(("groups", "cls"), None),
            P(("groups", "cls")),
            P(),
            P(("groups", "cls"), None, None, None),
            P(),
        ),
        out_specs=(P(("groups", "cls"), None, None, None), P(("groups", "cls"), None)),
        check_vma=False,
    )
```

```python
import functools
import math

import jax
import jax.numpy as jnp
import numpy as np
from jax import lax
from jax.experimental import pallas as pl
from jax.experimental.pallas import tpu as pltpu
from jax.sharding import PartitionSpec as P

SHIFT_GRID = ((-1, -1), (-1, 0), (-1, 1), (0, -1), (0, 0), (0, 1), (1, -1), (1, 0), (1, 1))
HALF_SHIFTS = SHIFT_GRID[5:]
SHIFTS = len(SHIFT_GRID)
MIB = 1 << 20

NT = (((1,), (1,)), ((), ()))
NN = (((1,), (0,)), ((), ()))


def dot(left, right, dims):
    return lax.dot_general(left, right, dims, preferred_element_type=jnp.float32)


def signed_frequencies(band):
    counter = np.arange(band)
    return np.where(counter < band // 2, counter, counter - band)


def fourier_table(box, band):
    angles = (signed_frequencies(band)[:, None] * np.arange(box)[None, :] % box) * (2.0 * math.pi / box)
    both = np.concatenate([np.cos(angles), np.sin(angles)], 0) / math.sqrt(box)
    return both.astype(np.float32).astype(jnp.bfloat16)


def shift_tables(band, box):
    frequency = signed_frequencies(band)
    u = np.array(HALF_SHIFTS)
    residue = frequency[None, :, None] * u[:, 0, None, None] + frequency[None, None, :] * u[:, 1, None, None]
    angles = (residue % box) * (2.0 * math.pi / box)
    return np.stack([np.cos(angles), np.sin(angles)], 1).astype(np.float32)


def cos_sin(steps, box):
    quarter = box // 4
    moved = (steps + quarter // 2) & (box - 1)
    turn = moved // quarter
    angle = ((moved & (quarter - 1)) - quarter // 2).astype(jnp.float32) * (2.0 * math.pi / box)
    sq = angle * angle
    c = 1.0 + sq * (-1 / 2 + sq * (1 / 24 + sq * (-1 / 720 + sq * (1 / 40320))))
    s = angle * (1.0 + sq * (-1 / 6 + sq * (1 / 120 + sq * (-1 / 5040 + sq * (1 / 362880)))))
    odd = (turn & 1) == 1
    cosine = jnp.where(odd, s, c)
    sine = jnp.where(odd, c, s)
    cosine = jnp.where((turn == 1) | (turn == 2), -cosine, cosine)
    sine = jnp.where(turn >= 2, -sine, sine)
    return cosine, sine


def iota_frequency(shape, dim):
    band = shape[dim]
    counter = lax.broadcasted_iota(jnp.int32, shape, dim)
    return jnp.where(counter < band // 2, counter, counter - band)


def spectra_kernel(grp_ref, off_ref, tile_ref, table_ref, contrast_ref, out_ref, stage, *, block):
    box = tile_ref.shape[-1]
    band = contrast_ref.shape[-1]
    first = pl.program_id(0) * block
    table = table_ref[...]
    count = off_ref.shape[1]
    lane = lax.broadcasted_iota(jnp.int32, (block, count), 1)
    place = lax.broadcasted_iota(jnp.int32, (block, count), 0) + first
    row_shift = jnp.sum(jnp.where(lane == place, off_ref[0:1, :], 0), 1, keepdims=True)
    col_shift = jnp.sum(jnp.where(lane == place, off_ref[1:2, :], 0), 1, keepdims=True)
    diagonal = lax.broadcasted_iota(jnp.int32, (block, block), 0) == lax.broadcasted_iota(
        jnp.int32, (block, block), 1
    )
    row_shift = jnp.sum(jnp.where(diagonal, row_shift, 0), 0, keepdims=True)
    row_cos, row_sin = cos_sin(iota_frequency((band, block), 0) * row_shift, box)
    col_cos, col_sin = cos_sin(iota_frequency((block, band), 1) * col_shift, box)
    for i in range(block):
        first_pass = dot(tile_ref[i], table, NT).astype(jnp.bfloat16)
        second = dot(table, first_pass, NN)
        re = (second[:band, :band] - second[band:, band:]).astype(jnp.bfloat16).astype(jnp.float32)
        im = (-(second[band:, :band] + second[:band, band:])).astype(jnp.bfloat16).astype(jnp.float32)
        rc = jnp.broadcast_to(row_cos[:, i : i + 1], (band, band))
        rs = jnp.broadcast_to(row_sin[:, i : i + 1], (band, band))
        cc, cs = col_cos[i : i + 1], col_sin[i : i + 1]
        gain = contrast_ref[grp_ref[first + i]].astype(jnp.float32)
        c = gain * (rc * cc - rs * cs)
        s = gain * (rs * cc + rc * cs)
        out_re = (c * re - s * im).astype(jnp.bfloat16).astype(jnp.float32)
        out_im = (c * im + s * re).astype(jnp.bfloat16).astype(jnp.float32)
        stage[0, pl.ds(i, band, stride=block), :] = out_re
        stage[1, pl.ds(i, band, stride=block), :] = out_im
    both = jnp.concatenate([stage[q].reshape(band, block, band) for q in range(2)], 1)
    out_ref[0] = both.reshape(band * 2 * block, band).astype(jnp.bfloat16)


def spectra(tiles, shifts, groups, table, contrast):
    count, box, _ = tiles.shape
    band = contrast.shape[-1]
    block = 8
    return pl.pallas_call(
        functools.partial(spectra_kernel, block=block),
        grid=(count // block,),
        out_shape=jax.ShapeDtypeStruct((count // block, band * 2 * block, band), jnp.bfloat16),
        in_specs=[
            pl.BlockSpec(memory_space=pltpu.SMEM),
            pl.BlockSpec(shifts.shape, lambda i: (0, 0)),
            pl.BlockSpec((block, box, box), lambda i: (i, 0, 0)),
            pl.BlockSpec(table.shape, lambda i: (0, 0)),
            pl.BlockSpec(contrast.shape, lambda i: (0, 0, 0)),
        ],
        out_specs=pl.BlockSpec((1, band * 2 * block, band), lambda i: (i, 0, 0)),
        scratch_shapes=[pltpu.VMEM((2, band * block, band), jnp.float32)],
        compiler_params=pltpu.CompilerParams(vmem_limit_bytes=62 * MIB),
        cost_estimate=pl.CostEstimate(
            flops=count * 4 * box**3, bytes_accessed=count * (box * box * 2 + band * band * 4), transcendentals=0
        ),
        name="spectra",
    )(groups, shifts, tiles, table, contrast)


def search_kernel(
    me_ref, list0_ref, list1_ref, class_ref, rot_ref, phase_ref, x0_ref, x1_ref, out_ref, ev_ref,
    work, left, shifted, score, diag, rot_t, partial_sum, weight_t, *, rots, half, chunk, group, order,
):
    band = rot_ref.shape[-1]
    wide = 2 * band
    pad = shifted.shape[1]
    own = list0_ref.shape[1]
    count = 2 * own
    blocks = x0_ref.shape[0]
    rows = band * chunk
    classes_step = 4

    @pl.when(pl.program_id(0) == 0)
    def _():
        diag[...] = jnp.zeros_like(diag)
        for r in range(rots):
            block = rot_ref[r * band : (r + 1) * band, :]
            diag[r, :band, :band] = block
            diag[r, band:, band:] = block
            rot_t[:, r * band : (r + 1) * band] = block.astype(jnp.float32).T.astype(jnp.bfloat16)

    for h in range(rots // half):

        @pl.loop(0, chunk // classes_step)
        def _(g):
            for k in range(classes_step):
                c = g * classes_step + k
                both = jnp.concatenate([class_ref[c, 0], class_ref[c, 1]], 1)
                halfway = dot(rot_ref[h * half * band : (h + 1) * half * band, :], both, NN)
                at = pl.ds(c, half * band, stride=chunk)
                left[0, at, :] = halfway[:, :band]
                left[1, at, :] = halfway[:, band:]

        @pl.loop(0, half // 2)
        def _(g):
            pair = []
            for k in range(2):
                r = g * 2 + k
                at = pl.ds(pl.multiple_of(r * rows, rows), rows)
                source = jnp.concatenate([left[0, at, :], left[1, at, :]], 1).astype(jnp.bfloat16)
                pair.append(dot(source, diag[h * half + r], NT).reshape(band, chunk, wide))
            turned = jnp.concatenate(pair, 1).reshape(2 * rows, wide).astype(jnp.bfloat16)
            work[pl.ds(pl.multiple_of((h * half // 2 + g) * 2 * rows, 2 * rows), 2 * rows), :] = turned

    cut = -(-pad // 32) * 16
    parts_of_rows = ((0, cut), (cut, pad))
    score[...] = jnp.zeros_like(score)

    @pl.loop(0, band // group)
    def _(g):
        ys, ts = [], []
        for k in range(group):
            j = g * group + k
            at = pl.ds(pl.multiple_of(j * 16, 16), 16)
            pairs = [ref[b, at, :].astype(jnp.float32) for ref in (x0_ref, x1_ref) for b in range(blocks)]
            re = jnp.concatenate([pair[:8] for pair in pairs], 0)
            im = jnp.concatenate([pair[8:] for pair in pairs], 0)
            parts = [None] * SHIFTS
            parts[SHIFTS // 2] = jnp.concatenate([re, im], 1)
            for s in range(len(HALF_SHIFTS)):
                c = phase_ref[s, 0, pl.ds(j, 1), :]
                d = phase_ref[s, 1, pl.ds(j, 1), :]
                cr, ci, dr, di = c * re, c * im, d * re, d * im
                parts[SHIFTS // 2 + 1 + s] = jnp.concatenate([cr - di, dr + ci], 1)
                parts[SHIFTS // 2 - 1 - s] = jnp.concatenate([cr + di, ci - dr], 1)
            if pad > SHIFTS * count:
                parts.append(jnp.zeros((pad - SHIFTS * count, wide), jnp.float32))
            y = jnp.concatenate(parts, 0).astype(jnp.bfloat16)
            shifted[j] = y
            ys.append(y)
            tiles = [pl.ds(pl.multiple_of(r * 2 * rows + j * 2 * chunk, 16), 2 * chunk) for r in range(rots // 2)]
            tiles += tiles[: max(0, 9 - len(tiles))]
            ts.append(jnp.concatenate([work[at, :] for at in tiles], 0))
        template_rows = jnp.concatenate(ts, 1)
        for low, high in parts_of_rows:
            score[low:high, :] += dot(jnp.concatenate([y[low:high] for y in ys], 1), template_rows, NT)

    base = pl.program_id(0) * chunk
    lane_class = lax.broadcasted_iota(jnp.int32, (count, rots * chunk), 1) & (chunk - 1)
    square = lax.broadcasted_iota(jnp.int32, (own, own), 0) == lax.broadcasted_iota(jnp.int32, (own, own), 1)
    masks_of = []
    for a in range(2):
        named = []
        for ref in (list0_ref, list1_ref):
            relative = ref[a : a + 1, :] ^ me_ref[0]
            slot = functools.reduce(jnp.add, [((relative >> bit) & 1) << t for t, bit in enumerate(order)])
            slot = jnp.where((relative & 1) == 0, slot - base, -1)
            named.append(jnp.sum(jnp.where(square, slot, 0), 1, keepdims=True))
        masks_of.append(lane_class == jnp.concatenate(named, 0))
    first, second = masks_of
    slabs = [score[s * count : (s + 1) * count, : rots * chunk] * (2.0 / band) for s in range(SHIFTS)]
    highest = functools.reduce(jnp.maximum, slabs)
    low = -3.0e38
    top0 = jnp.max(jnp.where(first, highest, low), 1, keepdims=True)
    top1 = jnp.max(jnp.where(second, highest, low), 1, keepdims=True)
    top = jnp.where(first, top0, top1)
    either = first | second
    exps = [jnp.where(either, jnp.exp(jnp.where(either, slab - top, 0.0)), 0.0) for slab in slabs]
    summed = functools.reduce(jnp.add, exps)
    total0 = jnp.sum(jnp.where(first, summed, 0.0), 1, keepdims=True)
    total1 = jnp.sum(jnp.where(second, summed, 0.0), 1, keepdims=True)
    here0 = total0 > 0.0
    here1 = total1 > 0.0
    total0 = jnp.where(here0, total0, 1.0)
    total1 = jnp.where(here1, total1, 1.0)
    total = jnp.where(first, total0, total1)
    weights = [e / total for e in exps]
    if pad > SHIFTS * count:
        weights.append(jnp.zeros((pad - SHIFTS * count, rots * chunk), jnp.float32))
    weight_t[...] = jnp.concatenate(weights, 0).T.astype(jnp.bfloat16)
    shiftless = math.log(rots * SHIFTS)
    for a, (there, top_a, total_a) in enumerate(((here0, top0, total0), (here1, top1, total1))):
        found = jnp.where(there, top_a + jnp.log(total_a) - shiftless, 0.0)
        for side in range(2):
            column = found[side * own : (side + 1) * own]
            row = jnp.sum(jnp.where(square, column, 0.0), 0, keepdims=True)
            at = (side, slice(a, a + 1))
            ev_ref[at] = row + jnp.where(pl.program_id(0) == 0, 0.0, ev_ref[at])

    @pl.loop(0, band // group)
    def _(g):
        for k in range(0, group, 2):
            j = g * group + k
            two = [dot(weight_t[...], shifted[j + i], NN).reshape(rots, chunk, wide) for i in range(2)]
            both = jnp.concatenate(two, 1).astype(jnp.bfloat16)
            for r in range(rots):
                work[pl.ds(pl.multiple_of(r * rows + j * chunk, 16), 2 * chunk), :] = both[r]

    for h in range(rots // half):

        @pl.loop(0, half // 2)
        def _(g):
            for k in range(2):
                r = g * 2 + k
                source = work[pl.ds(pl.multiple_of((h * half + r) * rows, rows), rows), :]
                turned = dot(source, diag[h * half + r], NN)
                at = pl.ds(pl.multiple_of(r * rows, rows), rows)
                left[0, at, :] = turned[:, :band]
                left[1, at, :] = turned[:, band:]

        @pl.loop(0, chunk // classes_step)
        def _(g):
            for k in range(classes_step):
                c = g * classes_step + k
                at = pl.ds(c, half * band, stride=chunk)
                column = jnp.concatenate([left[0, at, :], left[1, at, :]], 1).astype(jnp.bfloat16)
                turned = dot(rot_t[:, h * half * band : (h + 1) * half * band], column, NN)
                if h:
                    turned += partial_sum[c]
                if h < rots // half - 1:
                    partial_sum[c] = turned
                else:
                    out_ref[c, 0] = turned[:, :band].astype(jnp.bfloat16)
                    out_ref[c, 1] = turned[:, band:].astype(jnp.bfloat16)


def search(me, lists, classes, rotations, xs, order):
    n, _, band, _ = classes.shape
    wide = 2 * band
    rots = rotations.shape[0]
    own = lists[0].shape[1]
    chunk = 8
    half = rots // 2
    pad = -(-SHIFTS * 2 * own // 16) * 16
    phases = jnp.asarray(shift_tables(band, 2 * band))
    whole = lambda shape: pl.BlockSpec(shape, lambda i: (0,) * len(shape))
    classes_block = pl.BlockSpec((chunk, 2, band, band), lambda i: (i, 0, 0, 0))
    return pl.pallas_call(
        functools.partial(search_kernel, rots=rots, half=half, chunk=chunk, group=16, order=order),
        grid=(n // chunk,),
        out_shape=[
            jax.ShapeDtypeStruct((n, 2, band, band), jnp.bfloat16),
            jax.ShapeDtypeStruct((2, 2, own), jnp.float32),
        ],
        in_specs=[
            pl.BlockSpec(memory_space=pltpu.SMEM),
            whole((2, own)),
            whole((2, own)),
            classes_block,
            whole((rots * band, band)),
            whole(phases.shape),
            whole(xs[0].shape),
            whole(xs[1].shape),
        ],
        out_specs=[classes_block, whole((2, 2, own))],
        scratch_shapes=[
            pltpu.VMEM((rots * band * chunk, wide), jnp.bfloat16),
            pltpu.VMEM((2, half * band * chunk, band), jnp.float32),
            pltpu.VMEM((band, pad, wide), jnp.bfloat16),
            pltpu.VMEM((pad, max(rots, 18) * chunk), jnp.float32),
            pltpu.VMEM((rots, wide, wide), jnp.bfloat16),
            pltpu.VMEM((band, rots * band), jnp.bfloat16),
            pltpu.VMEM((chunk, band, wide), jnp.float32),
            pltpu.VMEM((rots * chunk, pad), jnp.bfloat16),
        ],
        compiler_params=pltpu.CompilerParams(vmem_limit_bytes=62 * MIB),
        cost_estimate=pl.CostEstimate(flops=10**10, bytes_accessed=10**7, transcendentals=0),
        name="search",
    )(me, *lists, classes, rotations.reshape(rots * band, band), phases, *xs)


def rounds(n):
    bits = list(range(n.bit_length() - 2, 0, -1))
    return [tuple(bits[i : i + 2]) for i in range(0, len(bits), 2)]


def masks(bits):
    count = len(bits)
    return [sum(((i >> t) & 1) << bits[count - 1 - t] for t in range(count)) for i in range(1, 1 << count)]


def swap(value, mask, n):
    return lax.ppermute(value, "cls", [(i, i ^ mask) for i in range(n)])


def on_device(tiles, class_lists, offsets, defocus_groups, contrast_table, references, rotations):
    n = lax.axis_size("cls")
    me = jnp.full((1,), lax.axis_index("cls"), jnp.int32)
    box = tiles.shape[-1]
    band = references.shape[-1]
    plan = rounds(n)
    order = [bit for bits in plan for bit in reversed(bits)]

    classes = references.astype(jnp.bfloat16)
    lists = class_lists.T
    lists = (lists, swap(lists, 1, n))
    x = spectra(tiles, offsets.T, defocus_groups, jnp.asarray(fourier_table(box, band)), contrast_table)
    for step, bits in enumerate(plan):
        classes = jnp.concatenate([classes] + [swap(classes, mask, n) for mask in masks(bits)], 0)
        if step == 0:
            classes, x = lax.optimization_barrier((classes, x))

    sums, evidence = search(me, lists, classes, rotations, (x, swap(x, 1, n)), order)

    evidence = evidence[0] + swap(evidence[1], 1, n)
    for bits in reversed(plan):
        parts = jnp.split(sums.astype(jnp.bfloat16), 1 << len(bits), 0)
        got = [swap(part, mask, n) for part, mask in zip(parts[1:], masks(bits))]
        sums = functools.reduce(jnp.add, [part.astype(jnp.float32) for part in parts[:1] + got])
    return sums, evidence.T


def solution(mesh):
    return jax.shard_map(
        on_device,
        mesh=mesh,
        in_specs=(
            P(("groups", "cls"), None, None),
            P(("groups", "cls"), None),
            P(("groups", "cls"), None),
            P(("groups", "cls")),
            P(),
            P(("groups", "cls"), None, None, None),
            P(),
        ),
        out_specs=(P(("groups", "cls"), None, None, None), P(("groups", "cls"), None)),
        check_vma=False,
    )
```

```python
import functools
import math

import jax
import jax.numpy as jnp
import numpy as np
from jax import lax
from jax.experimental import pallas as pl
from jax.experimental.pallas import tpu as pltpu
from jax.sharding import PartitionSpec as P

SHIFTS = 9
MIB = 1 << 20

NT = (((1,), (1,)), ((), ()))
NN = (((1,), (0,)), ((), ()))


def dot(left, right, dims):
    return lax.dot_general(left, right, dims, preferred_element_type=jnp.float32)


def signed_frequencies(band):
    counter = np.arange(band)
    return np.where(counter < band // 2, counter, counter - band)


def fourier_table(box, band):
    angles = (signed_frequencies(band)[:, None] * np.arange(box)[None, :] % box) * (2.0 * math.pi / box)
    both = np.concatenate([np.cos(angles), np.sin(angles)], 0) / math.sqrt(box)
    return both.astype(np.float32).astype(jnp.bfloat16)


def shift_tables(band, box):
    angles = signed_frequencies(band) * (2.0 * math.pi / box)
    both = []
    for values in (np.cos(angles), np.sin(angles)):
        by_row = np.repeat(np.broadcast_to(values[:, None], (band, band)), 8, 0)
        both.append(np.concatenate([by_row, np.broadcast_to(values[None, :], (8, band))], 0))
    return np.stack(both).astype(np.float32)


def cos_sin(steps, box):
    quarter = box // 4
    moved = (steps + quarter // 2) & (box - 1)
    turn = moved // quarter
    angle = ((moved & (quarter - 1)) - quarter // 2).astype(jnp.float32) * (2.0 * math.pi / box)
    sq = angle * angle
    c = 1.0 + sq * (-1 / 2 + sq * (1 / 24 + sq * (-1 / 720 + sq * (1 / 40320))))
    s = angle * (1.0 + sq * (-1 / 6 + sq * (1 / 120 + sq * (-1 / 5040 + sq * (1 / 362880)))))
    odd = (turn & 1) == 1
    cosine = jnp.where(odd, s, c)
    sine = jnp.where(odd, c, s)
    cosine = jnp.where((turn == 1) | (turn == 2), -cosine, cosine)
    sine = jnp.where(turn >= 2, -sine, sine)
    return cosine, sine


def iota_frequency(shape, dim):
    band = shape[dim]
    counter = lax.broadcasted_iota(jnp.int32, shape, dim)
    return jnp.where(counter < band // 2, counter, counter - band)


def spectra_kernel(grp_ref, off_ref, tile_ref, table_ref, contrast_ref, out_ref, stage, *, block):
    box = tile_ref.shape[-1]
    band = contrast_ref.shape[-1]
    first = pl.program_id(0) * block
    table = table_ref[...]
    count = off_ref.shape[1]
    lane = lax.broadcasted_iota(jnp.int32, (block, count), 1)
    place = lax.broadcasted_iota(jnp.int32, (block, count), 0) + first
    row_shift = jnp.sum(jnp.where(lane == place, off_ref[0:1, :], 0), 1, keepdims=True)
    col_shift = jnp.sum(jnp.where(lane == place, off_ref[1:2, :], 0), 1, keepdims=True)
    diagonal = lax.broadcasted_iota(jnp.int32, (block, block), 0) == lax.broadcasted_iota(
        jnp.int32, (block, block), 1
    )
    row_shift = jnp.sum(jnp.where(diagonal, row_shift, 0), 0, keepdims=True)
    row_cos, row_sin = cos_sin(iota_frequency((band, block), 0) * row_shift, box)
    col_cos, col_sin = cos_sin(iota_frequency((block, band), 1) * col_shift, box)
    for i in range(block):
        first_pass = dot(tile_ref[i], table, NT).astype(jnp.bfloat16)
        second = dot(table, first_pass, NN)
        re = (second[:band, :band] - second[band:, band:]).astype(jnp.bfloat16).astype(jnp.float32)
        im = (-(second[band:, :band] + second[:band, band:])).astype(jnp.bfloat16).astype(jnp.float32)
        rc = jnp.broadcast_to(row_cos[:, i : i + 1], (band, band))
        rs = jnp.broadcast_to(row_sin[:, i : i + 1], (band, band))
        cc, cs = col_cos[i : i + 1], col_sin[i : i + 1]
        gain = contrast_ref[grp_ref[first + i]].astype(jnp.float32)
        c = gain * (rc * cc - rs * cs)
        s = gain * (rs * cc + rc * cs)
        out_re = (c * re - s * im).astype(jnp.bfloat16).astype(jnp.float32)
        out_im = (c * im + s * re).astype(jnp.bfloat16).astype(jnp.float32)
        stage[0, pl.ds(i, band, stride=block), :] = out_re
        stage[1, pl.ds(i, band, stride=block), :] = out_im
    both = jnp.concatenate([stage[q].reshape(band, block, band) for q in range(2)], 1)
    out_ref[0] = both.reshape(band * 2 * block, band).astype(jnp.bfloat16)


def spectra(tiles, shifts, groups, table, contrast):
    count, box, _ = tiles.shape
    band = contrast.shape[-1]
    block = 8
    return pl.pallas_call(
        functools.partial(spectra_kernel, block=block),
        grid=(count // block,),
        out_shape=jax.ShapeDtypeStruct((count // block, band * 2 * block, band), jnp.bfloat16),
        in_specs=[
            pl.BlockSpec(memory_space=pltpu.SMEM),
            pl.BlockSpec(shifts.shape, lambda i: (0, 0)),
            pl.BlockSpec((block, box, box), lambda i: (i, 0, 0)),
            pl.BlockSpec(table.shape, lambda i: (0, 0)),
            pl.BlockSpec(contrast.shape, lambda i: (0, 0, 0)),
        ],
        out_specs=pl.BlockSpec((1, band * 2 * block, band), lambda i: (i, 0, 0)),
        scratch_shapes=[pltpu.VMEM((2, band * block, band), jnp.float32)],
        compiler_params=pltpu.CompilerParams(vmem_limit_bytes=62 * MIB),
        cost_estimate=pl.CostEstimate(
            flops=count * 4 * box**3, bytes_accessed=count * (box * box * 2 + band * band * 4), transcendentals=0
        ),
        name="spectra",
    )(groups, shifts, tiles, table, contrast)


def search_kernel(
    me_ref, list0_ref, list1_ref, class_ref, rot_ref, phase_ref, x0_ref, x1_ref, out_ref, ev_ref,
    work, left, shifted, score, diag, rot_t, weight, *, rots, chunk, group, order,
):
    band = rot_ref.shape[-1]
    wide = 2 * band
    own = list0_ref.shape[1]
    count = 2 * own
    blocks = x0_ref.shape[0]
    rows = band * chunk
    classes_step = 4
    places = rots * chunk

    @pl.when(pl.program_id(0) == 0)
    def _():
        diag[...] = jnp.zeros_like(diag)
        for r in range(rots):
            block = rot_ref[r * band : (r + 1) * band, :]
            diag[r, :band, :band] = block
            diag[r, band:, band:] = block
            rot_t[:, r * band : (r + 1) * band] = block.astype(jnp.float32).T.astype(jnp.bfloat16)

    @pl.loop(0, chunk // classes_step)
    def _(g):
        for k in range(classes_step):
            c = g * classes_step + k
            both = jnp.concatenate([class_ref[c, 0], class_ref[c, 1]], 1)
            halfway = dot(rot_ref[...], both, NN)
            at = pl.ds(c, rots * band, stride=chunk)
            left[0, at, :] = halfway[:, :band]
            left[1, at, :] = halfway[:, band:]

    @pl.loop(0, rots // 2)
    def _(g):
        turned = []
        for k in range(2):
            r = g * 2 + k
            at = pl.ds(pl.multiple_of(r * rows, rows), rows)
            source = jnp.concatenate([left[0, at, :], left[1, at, :]], 1).astype(jnp.bfloat16)
            rotated = dot(source, diag[r], NT)
            re, im = rotated[:, :band], rotated[:, band:]
            c, s = phase_ref[0, :rows, :], phase_ref[1, :rows, :]
            cr, ci, sr, si = c * re, c * im, s * re, s * im
            turned.append(((re, im), (cr + si, ci - sr), (cr - si, ci + sr)))
        for u in range(3):
            parts = [
                jnp.concatenate([turned[k][u][q].reshape(band, chunk, band) for k in range(2)], 1)
                .reshape(2 * rows, band)
                .astype(jnp.bfloat16)
                for q in range(2)
            ]
            at = pl.ds(pl.multiple_of((u * (rots // 2) + g) * 2 * rows, 2 * rows), 2 * rows)
            work[at, :] = jnp.concatenate(parts, 1)

    score[...] = jnp.zeros_like(score)

    @pl.loop(0, band // group)
    def _(g):
        ys, ts = [], []
        for k in range(group):
            j = g * group + k
            at = pl.ds(pl.multiple_of(j * 16, 16), 16)
            pairs = [ref[b, at, :].astype(jnp.float32) for ref in (x0_ref, x1_ref) for b in range(blocks)]
            re = jnp.concatenate([pair[:8] for pair in pairs], 0)
            im = jnp.concatenate([pair[8:] for pair in pairs], 0)
            c, s = phase_ref[0, rows : rows + 1, :], phase_ref[1, rows : rows + 1, :]
            cr, ci, sr, si = c * re, c * im, s * re, s * im
            y = jnp.concatenate(
                [jnp.concatenate(v, 1) for v in ((re, im), (cr - si, ci + sr), (cr + si, ci - sr))], 0
            ).astype(jnp.bfloat16)
            shifted[j] = y
            ys.append(y)
            tiles = [pl.ds(pl.multiple_of(r * 2 * rows + j * 2 * chunk, 16), 2 * chunk) for r in range(3 * rots // 2)]
            ts.append([work[at, :] for at in tiles])
        y = jnp.concatenate(ys, 1)
        cut = 3 * rots // 4
        for low, high in ((0, cut), (cut, 3 * rots // 2)):
            left_side = jnp.concatenate([jnp.concatenate(t[low:high], 0) for t in ts], 1)
            score[low * 2 * chunk : high * 2 * chunk, :] += dot(left_side, y, NT)

    groups = 3 * rots
    slabs = [score[i * chunk : (i + 1) * chunk, :] * (2.0 / band) for i in range(groups)]
    highest = functools.reduce(jnp.maximum, slabs)
    low = -3.0e38

    def over_shifts(op, row):
        joined = op(op(row[:, :count], row[:, count : 2 * count]), row[:, 2 * count :])
        return joined, jnp.concatenate([joined] * 3, 1)

    row_class = lax.broadcasted_iota(jnp.int32, (chunk, 3 * count), 0) + pl.program_id(0) * chunk
    named, tops, wide_tops = [], [], []
    for a in range(2):
        relative = jnp.concatenate([ref[a : a + 1, :] ^ me_ref[0] for ref in (list0_ref, list1_ref)], 1)
        slot = functools.reduce(jnp.add, [((relative >> bit) & 1) << t for t, bit in enumerate(order)])
        slot = jnp.where((relative & 1) == 0, slot, -1)
        named.append(row_class == jnp.concatenate([slot] * 3, 1))
        best = jnp.max(jnp.where(named[a], highest, low), 0, keepdims=True)
        top, wide_top = over_shifts(jnp.maximum, best)
        tops.append(top)
        wide_tops.append(wide_top)
    first, second = named
    either = first | second
    top = jnp.where(first, wide_tops[0], wide_tops[1])
    exps = [jnp.where(either, jnp.exp(jnp.where(either, slab - top, 0.0)), 0.0) for slab in slabs]
    summed = functools.reduce(jnp.add, exps)
    totals = []
    for a in range(2):
        partial = jnp.sum(jnp.where(named[a], summed, 0.0), 0, keepdims=True)
        total, wide_total = over_shifts(jnp.add, partial)
        totals.append(jnp.where(wide_total > 0.0, wide_total, 1.0))
        found = jnp.where(
            total > 0.0, tops[a] + jnp.log(jnp.where(total > 0.0, total, 1.0)) - math.log(rots * SHIFTS), 0.0
        )
        for side in range(2):
            at = (side, slice(a, a + 1))
            old = jnp.where(pl.program_id(0) == 0, 0.0, ev_ref[at])
            ev_ref[at] = found[:, side * own : (side + 1) * own] + old
    total = jnp.where(first, totals[0], totals[1])
    weight[...] = jnp.concatenate([e / total for e in exps], 0).astype(jnp.bfloat16)

    @pl.loop(0, band // group)
    def _(g):
        for k in range(0, group, 2):
            j = g * group + k
            two = []
            for i in range(2):
                gathered = dot(weight[...], shifted[j + i], NN)
                at = pl.ds(pl.multiple_of((j + i) * 8, 8), 8)
                c, s = phase_ref[0, at, :], phase_ref[1, at, :]
                still, plus, minus = [
                    gathered[u * places : (u + 1) * places].reshape(rots, chunk, wide) for u in range(3)
                ]
                total, change = plus + minus, plus - minus
                re = still[:, :, :band] + c * total[:, :, :band] - s * change[:, :, band:]
                im = still[:, :, band:] + c * total[:, :, band:] + s * change[:, :, :band]
                two.append((re, im))
            both = [jnp.concatenate([one[q] for one in two], 1).astype(jnp.bfloat16) for q in range(2)]
            for r in range(rots):
                at = pl.ds(pl.multiple_of(r * rows + j * chunk, 16), 2 * chunk)
                work[at, :] = jnp.concatenate([both[0][r], both[1][r]], 1)

    @pl.loop(0, rots // 2)
    def _(g):
        for k in range(2):
            r = g * 2 + k
            at = pl.ds(pl.multiple_of(r * rows, rows), rows)
            turned = dot(work[at, :], diag[r], NN)
            left[0, at, :] = turned[:, :band]
            left[1, at, :] = turned[:, band:]

    @pl.loop(0, chunk // classes_step)
    def _(g):
        for k in range(classes_step):
            c = g * classes_step + k
            at = pl.ds(c, rots * band, stride=chunk)
            column = jnp.concatenate([left[0, at, :], left[1, at, :]], 1).astype(jnp.bfloat16)
            turned = dot(rot_t[...], column, NN)
            out_ref[c, 0] = turned[:, :band].astype(jnp.bfloat16)
            out_ref[c, 1] = turned[:, band:].astype(jnp.bfloat16)


def search(me, lists, classes, rotations, xs, order):
    n, _, band, _ = classes.shape
    wide = 2 * band
    rots = rotations.shape[0]
    own = lists[0].shape[1]
    chunk = 8
    phases = jnp.asarray(shift_tables(band, 2 * band))
    whole = lambda shape: pl.BlockSpec(shape, lambda i: (0,) * len(shape))
    classes_block = pl.BlockSpec((chunk, 2, band, band), lambda i: (i, 0, 0, 0))
    return pl.pallas_call(
        functools.partial(search_kernel, rots=rots, chunk=chunk, group=32, order=order),
        grid=(n // chunk,),
        out_shape=[
            jax.ShapeDtypeStruct((n, 2, band, band), jnp.bfloat16),
            jax.ShapeDtypeStruct((2, 2, own), jnp.float32),
        ],
        in_specs=[
            pl.BlockSpec(memory_space=pltpu.SMEM),
            whole((2, own)),
            whole((2, own)),
            classes_block,
            whole((rots * band, band)),
            whole(phases.shape),
            whole(xs[0].shape),
            whole(xs[1].shape),
        ],
        out_specs=[classes_block, whole((2, 2, own))],
        scratch_shapes=[
            pltpu.VMEM((3 * rots * band * chunk, wide), jnp.bfloat16),
            pltpu.VMEM((2, rots * band * chunk, band), jnp.float32),
            pltpu.VMEM((band, 6 * own, wide), jnp.bfloat16),
            pltpu.VMEM((3 * rots * chunk, 6 * own), jnp.float32),
            pltpu.VMEM((rots, wide, wide), jnp.bfloat16),
            pltpu.VMEM((band, rots * band), jnp.bfloat16),
            pltpu.VMEM((3 * rots * chunk, 6 * own), jnp.bfloat16),
        ],
        compiler_params=pltpu.CompilerParams(vmem_limit_bytes=62 * MIB),
        cost_estimate=pl.CostEstimate(flops=10**10, bytes_accessed=10**7, transcendentals=0),
        name="search",
    )(me, *lists, classes, rotations.reshape(rots * band, band), phases, *xs)


def rounds(n):
    bits = list(range(n.bit_length() - 2, 0, -1))
    return [tuple(bits[i : i + 2]) for i in range(0, len(bits), 2)]


def masks(bits):
    count = len(bits)
    return [sum(((i >> t) & 1) << bits[count - 1 - t] for t in range(count)) for i in range(1, 1 << count)]


def swap(value, mask, n):
    return lax.ppermute(value, "cls", [(i, i ^ mask) for i in range(n)])


def on_device(tiles, class_lists, offsets, defocus_groups, contrast_table, references, rotations):
    n = lax.axis_size("cls")
    me = jnp.full((1,), lax.axis_index("cls"), jnp.int32)
    box = tiles.shape[-1]
    band = references.shape[-1]
    plan = rounds(n)
    order = [bit for bits in plan for bit in reversed(bits)]

    classes = references.astype(jnp.bfloat16)
    lists = class_lists.T
    lists = (lists, swap(lists, 1, n))
    x = spectra(tiles, offsets.T, defocus_groups, jnp.asarray(fourier_table(box, band)), contrast_table)
    for step, bits in enumerate(plan):
        classes = jnp.concatenate([classes] + [swap(classes, mask, n) for mask in masks(bits)], 0)
        if step == 0:
            classes, x = lax.optimization_barrier((classes, x))

    sums, evidence = search(me, lists, classes, rotations, (x, swap(x, 1, n)), order)

    evidence = evidence[0] + swap(evidence[1], 1, n)
    for bits in reversed(plan):
        parts = jnp.split(sums.astype(jnp.bfloat16), 1 << len(bits), 0)
        got = [swap(part, mask, n) for part, mask in zip(parts[1:], masks(bits))]
        sums = functools.reduce(jnp.add, [part.astype(jnp.float32) for part in parts[:1] + got])
    return sums, evidence.T


def solution(mesh):
    return jax.shard_map(
        on_device,
        mesh=mesh,
        in_specs=(
            P(("groups", "cls"), None, None),
            P(("groups", "cls"), None),
            P(("groups", "cls"), None),
            P(("groups", "cls")),
            P(),
            P(("groups", "cls"), None, None, None),
            P(),
        ),
        out_specs=(P(("groups", "cls"), None, None, None), P(("groups", "cls"), None)),
        check_vma=False,
    )
```

```python
import functools
import math

import jax
import jax.numpy as jnp
import numpy as np
from jax import lax
from jax.experimental import pallas as pl
from jax.experimental.pallas import tpu as pltpu
from jax.sharding import PartitionSpec as P

SHIFTS = 9
MIB = 1 << 20

NT = (((1,), (1,)), ((), ()))
NN = (((1,), (0,)), ((), ()))


def dot(left, right, dims):
    return lax.dot_general(left, right, dims, preferred_element_type=jnp.float32)


def signed_frequencies(band):
    counter = np.arange(band)
    return np.where(counter < band // 2, counter, counter - band)


def fourier_table(box, band):
    angles = (signed_frequencies(band)[:, None] * np.arange(box)[None, :] % box) * (2.0 * math.pi / box)
    both = np.concatenate([np.cos(angles), np.sin(angles)], 0) / math.sqrt(box)
    return both.astype(np.float32).astype(jnp.bfloat16)


def shift_tables(band, box):
    angles = signed_frequencies(band) * (2.0 * math.pi / box)
    both = []
    for values in (np.cos(angles), np.sin(angles)):
        by_row = np.repeat(np.broadcast_to(values[:, None], (band, band)), 8, 0)
        both.append(np.concatenate([by_row, np.broadcast_to(values[None, :], (8, band))], 0))
    return np.stack(both).astype(np.float32)


def cos_sin(steps, box):
    quarter = box // 4
    moved = (steps + quarter // 2) & (box - 1)
    turn = moved // quarter
    angle = ((moved & (quarter - 1)) - quarter // 2).astype(jnp.float32) * (2.0 * math.pi / box)
    sq = angle * angle
    c = 1.0 + sq * (-1 / 2 + sq * (1 / 24 + sq * (-1 / 720 + sq * (1 / 40320))))
    s = angle * (1.0 + sq * (-1 / 6 + sq * (1 / 120 + sq * (-1 / 5040 + sq * (1 / 362880)))))
    odd = (turn & 1) == 1
    cosine = jnp.where(odd, s, c)
    sine = jnp.where(odd, c, s)
    cosine = jnp.where((turn == 1) | (turn == 2), -cosine, cosine)
    sine = jnp.where(turn >= 2, -sine, sine)
    return cosine, sine


def iota_frequency(shape, dim):
    band = shape[dim]
    counter = lax.broadcasted_iota(jnp.int32, shape, dim)
    return jnp.where(counter < band // 2, counter, counter - band)


def spectra_kernel(grp_ref, off_ref, tile_ref, table_ref, contrast_ref, out_ref, stage, *, block, start):
    box = tile_ref.shape[-1]
    band = contrast_ref.shape[-1]
    first = (pl.program_id(0) + start) * block
    table = table_ref[...]
    count = off_ref.shape[1]
    lane = lax.broadcasted_iota(jnp.int32, (block, count), 1)
    place = lax.broadcasted_iota(jnp.int32, (block, count), 0) + first
    row_shift = jnp.sum(jnp.where(lane == place, off_ref[0:1, :], 0), 1, keepdims=True)
    col_shift = jnp.sum(jnp.where(lane == place, off_ref[1:2, :], 0), 1, keepdims=True)
    diagonal = lax.broadcasted_iota(jnp.int32, (block, block), 0) == lax.broadcasted_iota(
        jnp.int32, (block, block), 1
    )
    row_shift = jnp.sum(jnp.where(diagonal, row_shift, 0), 0, keepdims=True)
    row_cos, row_sin = cos_sin(iota_frequency((band, block), 0) * row_shift, box)
    col_cos, col_sin = cos_sin(iota_frequency((block, band), 1) * col_shift, box)
    for i in range(block):
        first_pass = dot(tile_ref[i], table, NT).astype(jnp.bfloat16)
        second = dot(table, first_pass, NN)
        re = (second[:band, :band] - second[band:, band:]).astype(jnp.bfloat16).astype(jnp.float32)
        im = (-(second[band:, :band] + second[:band, band:])).astype(jnp.bfloat16).astype(jnp.float32)
        rc = jnp.broadcast_to(row_cos[:, i : i + 1], (band, band))
        rs = jnp.broadcast_to(row_sin[:, i : i + 1], (band, band))
        cc, cs = col_cos[i : i + 1], col_sin[i : i + 1]
        gain = contrast_ref[grp_ref[first + i]].astype(jnp.float32)
        c = gain * (rc * cc - rs * cs)
        s = gain * (rs * cc + rc * cs)
        out_re = (c * re - s * im).astype(jnp.bfloat16).astype(jnp.float32)
        out_im = (c * im + s * re).astype(jnp.bfloat16).astype(jnp.float32)
        stage[0, pl.ds(i, band, stride=block), :] = out_re
        stage[1, pl.ds(i, band, stride=block), :] = out_im
    both = jnp.concatenate([stage[q].reshape(band, block, band) for q in range(2)], 1)
    out_ref[0] = both.reshape(band * 2 * block, band).astype(jnp.bfloat16)


def spectra(tiles, shifts, groups, table, contrast, start, blocks):
    _, box, _ = tiles.shape
    band = contrast.shape[-1]
    block = 8
    count = blocks * block
    return pl.pallas_call(
        functools.partial(spectra_kernel, block=block, start=start),
        grid=(blocks,),
        out_shape=jax.ShapeDtypeStruct((blocks, band * 2 * block, band), jnp.bfloat16),
        in_specs=[
            pl.BlockSpec(memory_space=pltpu.SMEM),
            pl.BlockSpec(shifts.shape, lambda i: (0, 0)),
            pl.BlockSpec((block, box, box), lambda i: (i + start, 0, 0)),
            pl.BlockSpec(table.shape, lambda i: (0, 0)),
            pl.BlockSpec(contrast.shape, lambda i: (0, 0, 0)),
        ],
        out_specs=pl.BlockSpec((1, band * 2 * block, band), lambda i: (i, 0, 0)),
        scratch_shapes=[pltpu.VMEM((2, band * block, band), jnp.float32)],
        compiler_params=pltpu.CompilerParams(vmem_limit_bytes=62 * MIB),
        cost_estimate=pl.CostEstimate(
            flops=count * 4 * box**3, bytes_accessed=count * (box * box * 2 + band * band * 4), transcendentals=0
        ),
        name="spectra",
    )(groups, shifts, tiles, table, contrast)


def search_kernel(
    me_ref, list0_ref, list1_ref, rot_ref, phase_hbm, *refs, rots, chunk, group, order, n_classes, n_x,
):
    class_refs, refs = refs[:n_classes], refs[n_classes:]
    x_hbm, refs = refs[:n_x], refs[n_x:]
    out_refs, refs = refs[:n_classes], refs[n_classes:]
    ev_ref, work, left, shifted, score, diag, rot_t, weight, x_ref, phase_ref, x_sems, phase_sem = refs
    band = rot_ref.shape[-1]
    wide = 2 * band
    own = list0_ref.shape[1]
    count = 2 * own
    blocks = x_ref.shape[0]
    rows = band * chunk
    class_at = [(i, k) for i, ref in enumerate(class_refs) for k in range(ref.shape[0])]

    starts = [sum(ref.shape[0] for ref in x_hbm[:i]) for i in range(n_x)]
    copies = [
        pltpu.make_async_copy(ref, x_ref.at[pl.ds(starts[i], ref.shape[0])], x_sems.at[i])
        for i, ref in enumerate(x_hbm)
    ]
    phase_copy = pltpu.make_async_copy(phase_hbm, phase_ref, phase_sem)

    @pl.when(pl.program_id(0) == 0)
    def _():
        phase_copy.start()
        for copy in copies:
            copy.start()
        diag[...] = jnp.zeros_like(diag)
        for r in range(rots):
            block = rot_ref[r * band : (r + 1) * band, :]
            diag[r, :band, :band] = block
            diag[r, band:, band:] = block
            rot_t[:, r * band : (r + 1) * band] = block.astype(jnp.float32).T.astype(jnp.bfloat16)

    for c, (i, k) in enumerate(class_at):
        both = jnp.concatenate([class_refs[i][k, 0], class_refs[i][k, 1]], 1)
        halfway = dot(rot_ref[...], both, NN)
        at = pl.ds(c, rots * band, stride=chunk)
        left[0, at, :] = halfway[:, :band]
        left[1, at, :] = halfway[:, band:]

    @pl.when(pl.program_id(0) == 0)
    def _():
        phase_copy.wait()

    def paired(one, other):
        joined = [
            jnp.concatenate([half[q].reshape(band, chunk, band) for half in (one, other)], 1)
            .reshape(2 * rows, band)
            .astype(jnp.bfloat16)
            for q in range(2)
        ]
        return jnp.concatenate(joined, 1)

    @pl.loop(0, rots // 2)
    def _(g):
        def place(t):
            return pl.ds(pl.multiple_of((g * 3 + t) * 2 * rows, 2 * rows), 2 * rows)

        still = []
        for k in range(2):
            r = g * 2 + k
            at = pl.ds(pl.multiple_of(r * rows, rows), rows)
            source = jnp.concatenate([left[0, at, :], left[1, at, :]], 1).astype(jnp.bfloat16)
            rotated = dot(source, diag[r], NT)
            re, im = rotated[:, :band], rotated[:, band:]
            c, s = phase_ref[0, :rows, :], phase_ref[1, :rows, :]
            cr, ci, sr, si = c * re, c * im, s * re, s * im
            work[place(1 + k), :] = paired((cr + si, ci - sr), (cr - si, ci + sr))
            still.append((re, im))
        work[place(0), :] = paired(*still)

    @pl.when(pl.program_id(0) == 0)
    def _():
        for copy in copies:
            copy.wait()

    score[...] = jnp.zeros_like(score)

    @pl.loop(0, band // group)
    def _(g):
        ys, ts = [], []
        for k in range(group):
            j = g * group + k
            at = pl.ds(pl.multiple_of(j * 16, 16), 16)
            pairs = [x_ref[b, at, :].astype(jnp.float32) for b in range(blocks)]
            re = jnp.concatenate([pair[:8] for pair in pairs], 0)
            im = jnp.concatenate([pair[8:] for pair in pairs], 0)
            c, s = phase_ref[0, rows : rows + 1, :], phase_ref[1, rows : rows + 1, :]
            cr, ci, sr, si = c * re, c * im, s * re, s * im
            y = jnp.concatenate(
                [jnp.concatenate(v, 1) for v in ((re, im), (cr - si, ci + sr), (cr + si, ci - sr))], 0
            ).astype(jnp.bfloat16)
            shifted[j] = y
            ys.append(y)
            tiles = [pl.ds(pl.multiple_of(r * 2 * rows + j * 2 * chunk, 16), 2 * chunk) for r in range(3 * rots // 2)]
            ts.append([work[at, :] for at in tiles])
        y = jnp.concatenate(ys, 1)
        cut = 3 * rots // 4
        for low, high in ((0, cut), (cut, 3 * rots // 2)):
            left_side = jnp.concatenate([jnp.concatenate(t[low:high], 0) for t in ts], 1)
            score[low * 2 * chunk : high * 2 * chunk, :] += dot(left_side, y, NT)

    groups = 3 * rots
    slabs = [score[i * chunk : (i + 1) * chunk, :] * (2.0 / band) for i in range(groups)]
    highest = functools.reduce(jnp.maximum, slabs)
    low = -3.0e38

    def over_shifts(op, row):
        joined = op(op(row[:, :count], row[:, count : 2 * count]), row[:, 2 * count :])
        return joined, jnp.concatenate([joined] * 3, 1)

    row_class = lax.broadcasted_iota(jnp.int32, (chunk, 3 * count), 0) + pl.program_id(0) * chunk
    named, tops, wide_tops = [], [], []
    for a in range(2):
        relative = jnp.concatenate([ref[a : a + 1, :] ^ me_ref[0] for ref in (list0_ref, list1_ref)], 1)
        slot = functools.reduce(jnp.add, [((relative >> bit) & 1) << t for t, bit in enumerate(order)])
        slot = jnp.where((relative & 1) == 0, slot, -1)
        named.append(row_class == jnp.concatenate([slot] * 3, 1))
        best = jnp.max(jnp.where(named[a], highest, low), 0, keepdims=True)
        top, wide_top = over_shifts(jnp.maximum, best)
        tops.append(top)
        wide_tops.append(wide_top)
    first, second = named
    either = first | second
    top = jnp.where(first, wide_tops[0], wide_tops[1])
    exps = [jnp.where(either, jnp.exp(jnp.where(either, slab - top, 0.0)), 0.0) for slab in slabs]
    summed = functools.reduce(jnp.add, exps)
    totals = []
    for a in range(2):
        partial = jnp.sum(jnp.where(named[a], summed, 0.0), 0, keepdims=True)
        total, wide_total = over_shifts(jnp.add, partial)
        totals.append(jnp.where(wide_total > 0.0, wide_total, 1.0))
        found = jnp.where(
            total > 0.0, tops[a] + jnp.log(jnp.where(total > 0.0, total, 1.0)) - math.log(rots * SHIFTS), 0.0
        )
        for side in range(2):
            at = (side, slice(a, a + 1))
            old = jnp.where(pl.program_id(0) == 0, 0.0, ev_ref[at])
            ev_ref[at] = found[:, side * own : (side + 1) * own] + old
    total = jnp.where(first, totals[0], totals[1])
    weight[...] = jnp.concatenate([e / total for e in exps], 0).astype(jnp.bfloat16)

    @pl.loop(0, band // group)
    def _(g):
        for k in range(0, group, 2):
            j = g * group + k
            two = []
            for i in range(2):
                gathered = dot(weight[...], shifted[j + i], NN)
                at = pl.ds(pl.multiple_of((j + i) * 8, 8), 8)
                c, s = phase_ref[0, at, :], phase_ref[1, at, :]
                tiled = gathered.reshape(rots // 2, 3, 2, chunk, wide)
                still = tiled[:, 0].reshape(rots, chunk, wide)
                plus = tiled[:, 1:, 0].reshape(rots, chunk, wide)
                minus = tiled[:, 1:, 1].reshape(rots, chunk, wide)
                total, change = plus + minus, plus - minus
                re = still[:, :, :band] + c * total[:, :, :band] - s * change[:, :, band:]
                im = still[:, :, band:] + c * total[:, :, band:] + s * change[:, :, :band]
                two.append((re, im))
            both = [jnp.concatenate([one[q] for one in two], 1).astype(jnp.bfloat16) for q in range(2)]
            for r in range(rots):
                at = pl.ds(pl.multiple_of(r * rows + j * chunk, 16), 2 * chunk)
                work[at, :] = jnp.concatenate([both[0][r], both[1][r]], 1)

    @pl.loop(0, rots // 2)
    def _(g):
        for k in range(2):
            r = g * 2 + k
            at = pl.ds(pl.multiple_of(r * rows, rows), rows)
            turned = dot(work[at, :], diag[r], NN)
            left[0, at, :] = turned[:, :band]
            left[1, at, :] = turned[:, band:]

    for c, (i, k) in enumerate(class_at):
        at = pl.ds(c, rots * band, stride=chunk)
        column = jnp.concatenate([left[0, at, :], left[1, at, :]], 1).astype(jnp.bfloat16)
        turned = dot(rot_t[...], column, NN)
        out_refs[i][k, 0] = turned[:, :band].astype(jnp.bfloat16)
        out_refs[i][k, 1] = turned[:, band:].astype(jnp.bfloat16)


def search(me, lists, classes, rotations, xs, order):
    band = classes[0].shape[-1]
    wide = 2 * band
    rots = rotations.shape[0]
    own = lists[0].shape[1]
    chunk = 8
    n = sum(a.shape[0] for a in classes)
    sizes = [a.shape[0] for a in classes] if n == chunk else [chunk]
    phases = jnp.asarray(shift_tables(band, 2 * band))
    whole = lambda shape: pl.BlockSpec(shape, lambda i: (0,) * len(shape))
    apart = pl.BlockSpec(memory_space=pl.ANY)
    class_blocks = [pl.BlockSpec((size, 2, band, band), lambda i: (i, 0, 0, 0)) for size in sizes]
    *sums, evidence = pl.pallas_call(
        functools.partial(
            search_kernel, rots=rots, chunk=chunk, group=32, order=order, n_classes=len(classes), n_x=len(xs)
        ),
        grid=(n // chunk,),
        out_shape=[jax.ShapeDtypeStruct(a.shape, jnp.bfloat16) for a in classes]
        + [jax.ShapeDtypeStruct((2, 2, own), jnp.float32)],
        in_specs=[
            pl.BlockSpec(memory_space=pltpu.SMEM),
            whole((2, own)),
            whole((2, own)),
            whole((rots * band, band)),
            apart,
        ]
        + class_blocks
        + [apart] * len(xs),
        out_specs=class_blocks + [whole((2, 2, own))],
        scratch_shapes=[
            pltpu.VMEM((3 * rots * band * chunk, wide), jnp.bfloat16),
            pltpu.VMEM((2, rots * band * chunk, band), jnp.float32),
            pltpu.VMEM((band, 6 * own, wide), jnp.bfloat16),
            pltpu.VMEM((3 * rots * chunk, 6 * own), jnp.float32),
            pltpu.VMEM((rots, wide, wide), jnp.bfloat16),
            pltpu.VMEM((band, rots * band), jnp.bfloat16),
            pltpu.VMEM((3 * rots * chunk, 6 * own), jnp.bfloat16),
            pltpu.VMEM((sum(x.shape[0] for x in xs),) + xs[0].shape[1:], jnp.bfloat16),
            pltpu.VMEM(phases.shape, jnp.float32),
            pltpu.SemaphoreType.DMA((len(xs),)),
            pltpu.SemaphoreType.DMA,
        ],
        compiler_params=pltpu.CompilerParams(vmem_limit_bytes=62 * MIB),
        cost_estimate=pl.CostEstimate(flops=10**10, bytes_accessed=10**7, transcendentals=0),
        name="search",
    )(me, *lists, rotations.reshape(rots * band, band), phases, *classes, *xs)
    return sums, evidence


def rounds(n):
    bits = list(range(n.bit_length() - 2, 0, -1))
    return [tuple(bits[i : i + 2]) for i in range(0, len(bits), 2)]


def masks(bits):
    count = len(bits)
    return [sum(((i >> t) & 1) << bits[count - 1 - t] for t in range(count)) for i in range(1, 1 << count)]


def swap(value, mask, n):
    return lax.ppermute(value, "cls", [(i, i ^ mask) for i in range(n)])


def on_device(tiles, class_lists, offsets, defocus_groups, contrast_table, references, rotations):
    n = lax.axis_size("cls")
    me = jnp.full((1,), lax.axis_index("cls"), jnp.int32)
    box = tiles.shape[-1]
    band = references.shape[-1]
    plan = rounds(n)
    order = [bit for bits in plan for bit in reversed(bits)]

    mine = references.astype(jnp.bfloat16)
    lists = class_lists.T
    lists = (lists, swap(lists, 1, n))
    shifts = offsets.T
    table = jnp.asarray(fourier_table(box, band))
    blocks = tiles.shape[0] // 8
    before = blocks * 2 // 3

    near = masks(plan[0])
    if len(plan) == 2 and len(plan[1]) == 1:
        across = masks(plan[1])[0]
        others = [swap(mine, mask, n) for mask in near]
        facing = swap(mine, across, n)
        x0 = spectra(tiles, shifts, defocus_groups, table, contrast_table, 0, before)
        others, facing, x0, shifts = lax.optimization_barrier((others, facing, x0, shifts))
        others = jnp.concatenate(others, 0)
        classes = [mine, others, facing, swap(others, across, n)]
    else:
        x0 = spectra(tiles, shifts, defocus_groups, table, contrast_table, 0, before)
        for bits in plan:
            mine = jnp.concatenate([mine] + [swap(mine, mask, n) for mask in masks(bits)], 0)
        classes = [mine]
    x1 = spectra(tiles, shifts, defocus_groups, table, contrast_table, before, blocks - before)
    xs = (x0, x1, swap(x0, 1, n), swap(x1, 1, n))

    sums, evidence = search(me, lists, classes, rotations, xs, order)

    evidence = evidence[0] + swap(evidence[1], 1, n)
    if len(classes) == 4:
        mine, others, facing, given = sums
        arrived = swap(given, across, n)
        facing, arrived = lax.optimization_barrier((facing, arrived))
        others = (others.astype(jnp.float32) + arrived.astype(jnp.float32)).astype(jnp.bfloat16)
        got = [swap(part, mask, n) for part, mask in zip(jnp.split(others, len(near), 0), near)]
        got.append(swap(facing, across, n))
        sums = functools.reduce(jnp.add, [part.astype(jnp.float32) for part in [mine] + got])
    else:
        sums = sums[0]
        for bits in reversed(plan):
            parts = jnp.split(sums.astype(jnp.bfloat16), 1 << len(bits), 0)
            got = [swap(part, mask, n) for part, mask in zip(parts[1:], masks(bits))]
            sums = functools.reduce(jnp.add, [part.astype(jnp.float32) for part in parts[:1] + got])
    return sums, evidence.T


def solution(mesh):
    return jax.shard_map(
        on_device,
        mesh=mesh,
        in_specs=(
            P(("groups", "cls"), None, None),
            P(("groups", "cls"), None),
            P(("groups", "cls"), None),
            P(("groups", "cls")),
            P(),
            P(("groups", "cls"), None, None, None),
            P(),
        ),
        out_specs=(P(("groups", "cls"), None, None, None), P(("groups", "cls"), None)),
        check_vma=False,
    )
```

```python
import functools
import math

import jax
import jax.numpy as jnp
import numpy as np
from jax import lax
from jax.experimental import pallas as pl
from jax.experimental.pallas import tpu as pltpu
from jax.sharding import PartitionSpec as P

SHIFTS = 9
MIB = 1 << 20

NT = (((1,), (1,)), ((), ()))
NN = (((1,), (0,)), ((), ()))


def dot(left, right, dims):
    return lax.dot_general(left, right, dims, preferred_element_type=jnp.float32)


def signed_frequencies(band):
    counter = np.arange(band)
    return np.where(counter < band // 2, counter, counter - band)


def fourier_table(box, band):
    angles = (signed_frequencies(band)[:, None] * np.arange(box)[None, :] % box) * (2.0 * math.pi / box)
    both = np.concatenate([np.cos(angles), np.sin(angles)], 0) / math.sqrt(box)
    return both.astype(np.float32).astype(jnp.bfloat16)


def shift_tables(band, box):
    angles = signed_frequencies(band) * (2.0 * math.pi / box)
    both = []
    for values in (np.cos(angles), np.sin(angles)):
        by_row = np.repeat(np.broadcast_to(values[:, None], (band, band)), 8, 0)
        both.append(np.concatenate([by_row, np.broadcast_to(values[None, :], (8, band))], 0))
    return np.stack(both).astype(np.float32)


def cos_sin(steps, box):
    quarter = box // 4
    moved = (steps + quarter // 2) & (box - 1)
    turn = moved // quarter
    angle = ((moved & (quarter - 1)) - quarter // 2).astype(jnp.float32) * (2.0 * math.pi / box)
    sq = angle * angle
    c = 1.0 + sq * (-1 / 2 + sq * (1 / 24 + sq * (-1 / 720 + sq * (1 / 40320))))
    s = angle * (1.0 + sq * (-1 / 6 + sq * (1 / 120 + sq * (-1 / 5040 + sq * (1 / 362880)))))
    odd = (turn & 1) == 1
    cosine = jnp.where(odd, s, c)
    sine = jnp.where(odd, c, s)
    cosine = jnp.where((turn == 1) | (turn == 2), -cosine, cosine)
    sine = jnp.where(turn >= 2, -sine, sine)
    return cosine, sine


def iota_frequency(shape, dim):
    band = shape[dim]
    counter = lax.broadcasted_iota(jnp.int32, shape, dim)
    return jnp.where(counter < band // 2, counter, counter - band)


def spectra_kernel(grp_ref, off_ref, list_ref, tile_ref, table_ref, contrast_ref, out_ref, stage, *, block, start):
    box = tile_ref.shape[-1]
    band = contrast_ref.shape[-1]
    first = (pl.program_id(0) + start) * block
    table = table_ref[...]
    count = off_ref.shape[1]
    lane = lax.broadcasted_iota(jnp.int32, (block, count), 1)
    place = lax.broadcasted_iota(jnp.int32, (block, count), 0) + first
    row_shift = jnp.sum(jnp.where(lane == place, off_ref[0:1, :], 0), 1, keepdims=True)
    col_shift = jnp.sum(jnp.where(lane == place, off_ref[1:2, :], 0), 1, keepdims=True)
    diagonal = lax.broadcasted_iota(jnp.int32, (block, block), 0) == lax.broadcasted_iota(
        jnp.int32, (block, block), 1
    )
    row_shift = jnp.sum(jnp.where(diagonal, row_shift, 0), 0, keepdims=True)
    row_cos, row_sin = cos_sin(iota_frequency((band, block), 0) * row_shift, box)
    col_cos, col_sin = cos_sin(iota_frequency((block, band), 1) * col_shift, box)
    for i in range(block):
        first_pass = dot(tile_ref[i], table, NT).astype(jnp.bfloat16)
        second = dot(table, first_pass, NN)
        re = (second[:band, :band] - second[band:, band:]).astype(jnp.bfloat16).astype(jnp.float32)
        im = (-(second[band:, :band] + second[:band, band:])).astype(jnp.bfloat16).astype(jnp.float32)
        rc = jnp.broadcast_to(row_cos[:, i : i + 1], (band, band))
        rs = jnp.broadcast_to(row_sin[:, i : i + 1], (band, band))
        cc, cs = col_cos[i : i + 1], col_sin[i : i + 1]
        gain = contrast_ref[grp_ref[first + i]].astype(jnp.float32)
        c = gain * (rc * cc - rs * cs)
        s = gain * (rs * cc + rc * cs)
        out_re = (c * re - s * im).astype(jnp.bfloat16).astype(jnp.float32)
        out_im = (c * im + s * re).astype(jnp.bfloat16).astype(jnp.float32)
        stage[0, pl.ds(i, band, stride=block), :] = out_re
        stage[1, pl.ds(i, band, stride=block), :] = out_im
    both = jnp.concatenate([stage[q].reshape(band, block, band) for q in range(2)], 1)
    out_ref[0, : band * 2 * block, :] = both.reshape(band * 2 * block, band).astype(jnp.bfloat16)
    lists = jnp.concatenate([list_ref[...].astype(jnp.float32), jnp.zeros((14, count), jnp.float32)], 0)
    lists = jnp.concatenate([lists, jnp.zeros((16, band - count), jnp.float32)], 1)
    out_ref[0, band * 2 * block :, :] = lists.astype(jnp.bfloat16)


def spectra(tiles, shifts, lists, groups, table, contrast, start, blocks):
    _, box, _ = tiles.shape
    band = contrast.shape[-1]
    block = 8
    count = blocks * block
    return pl.pallas_call(
        functools.partial(spectra_kernel, block=block, start=start),
        grid=(blocks,),
        out_shape=jax.ShapeDtypeStruct((blocks, band * 2 * block + 16, band), jnp.bfloat16),
        in_specs=[
            pl.BlockSpec(memory_space=pltpu.SMEM),
            pl.BlockSpec(shifts.shape, lambda i: (0, 0)),
            pl.BlockSpec(lists.shape, lambda i: (0, 0)),
            pl.BlockSpec((block, box, box), lambda i: (i + start, 0, 0)),
            pl.BlockSpec(table.shape, lambda i: (0, 0)),
            pl.BlockSpec(contrast.shape, lambda i: (0, 0, 0)),
        ],
        out_specs=pl.BlockSpec((1, band * 2 * block + 16, band), lambda i: (i, 0, 0)),
        scratch_shapes=[pltpu.VMEM((2, band * block, band), jnp.float32)],
        compiler_params=pltpu.CompilerParams(vmem_limit_bytes=62 * MIB),
        cost_estimate=pl.CostEstimate(
            flops=count * 4 * box**3, bytes_accessed=count * (box * box * 2 + band * band * 4), transcendentals=0
        ),
        name="spectra",
    )(groups, shifts, lists, tiles, table, contrast)


def search_kernel(
    me_ref, list_ref, rot_ref, phase_hbm, x_hbm, *refs, rots, chunk, group, order, n_classes,
):
    class_refs, refs = refs[:n_classes], refs[n_classes:]
    out_refs, refs = refs[:n_classes], refs[n_classes:]
    ev_ref, work, left, shifted, score, diag, rot_t, weight, phase_ref, x_ref, phase_sem, x_sem = refs
    band = rot_ref.shape[-1]
    wide = 2 * band
    own = list_ref.shape[1]
    count = 2 * own
    rows = band * chunk
    class_at = [(i, k) for i, ref in enumerate(class_refs) for k in range(ref.shape[0])]

    phase_copy = pltpu.make_async_copy(phase_hbm, phase_ref, phase_sem)
    x_copy = pltpu.make_async_copy(x_hbm, x_ref, x_sem)
    blocks = x_ref.shape[0]

    @pl.when(pl.program_id(0) == 0)
    def _():
        phase_copy.start()
        x_copy.start()
        diag[...] = jnp.zeros_like(diag)
        for r in range(rots):
            block = rot_ref[r * band : (r + 1) * band, :]
            diag[r, :band, :band] = block
            diag[r, band:, band:] = block
            rot_t[:, r * band : (r + 1) * band] = block.astype(jnp.float32).T.astype(jnp.bfloat16)

    for c, (i, k) in enumerate(class_at):
        both = jnp.concatenate([class_refs[i][k, 0], class_refs[i][k, 1]], 1)
        halfway = dot(rot_ref[...], both, NN)
        at = pl.ds(c, rots * band, stride=chunk)
        left[0, at, :] = halfway[:, :band]
        left[1, at, :] = halfway[:, band:]

    @pl.when(pl.program_id(0) == 0)
    def _():
        phase_copy.wait()

    def paired(one, other):
        joined = [
            jnp.concatenate([half[q].reshape(band, chunk, band) for half in (one, other)], 1)
            .reshape(2 * rows, band)
            .astype(jnp.bfloat16)
            for q in range(2)
        ]
        return jnp.concatenate(joined, 1)

    @pl.loop(0, rots // 2, unroll=2)
    def _(g):
        def place(t):
            return pl.ds(pl.multiple_of((g * 3 + t) * 2 * rows, 2 * rows), 2 * rows)

        still = []
        for k in range(2):
            r = g * 2 + k
            at = pl.ds(pl.multiple_of(r * rows, rows), rows)
            source = jnp.concatenate([left[0, at, :], left[1, at, :]], 1).astype(jnp.bfloat16)
            rotated = dot(source, diag[r], NT)
            re, im = rotated[:, :band], rotated[:, band:]
            c, s = phase_ref[0, :rows, :], phase_ref[1, :rows, :]
            cr, ci, sr, si = c * re, c * im, s * re, s * im
            work[place(1 + k), :] = paired((cr + si, ci - sr), (cr - si, ci + sr))
            still.append((re, im))
        work[place(0), :] = paired(*still)

    @pl.when(pl.program_id(0) == 0)
    def _():
        x_copy.wait()

    score[...] = jnp.zeros_like(score)

    @pl.loop(0, band // group)
    def _(g):
        ys, ts = [], []
        for k in range(group):
            j = g * group + k
            at = pl.ds(pl.multiple_of(j * 16, 16), 16)
            pairs = [x_ref[b, at, :].astype(jnp.float32) for b in range(blocks)]
            re = jnp.concatenate([pair[:8] for pair in pairs], 0)
            im = jnp.concatenate([pair[8:] for pair in pairs], 0)
            c, s = phase_ref[0, rows : rows + 1, :], phase_ref[1, rows : rows + 1, :]
            cr, ci, sr, si = c * re, c * im, s * re, s * im
            y = jnp.concatenate(
                [jnp.concatenate(v, 1) for v in ((re, im), (cr - si, ci + sr), (cr + si, ci - sr))], 0
            ).astype(jnp.bfloat16)
            shifted[j] = y
            ys.append(y)
            tiles = [pl.ds(pl.multiple_of(r * 2 * rows + j * 2 * chunk, 16), 2 * chunk) for r in range(3 * rots // 2)]
            ts.append([work[at, :] for at in tiles])
        y = jnp.concatenate(ys, 1)
        cut = 3 * rots // 4
        for low, high in ((0, cut), (cut, 3 * rots // 2)):
            left_side = jnp.concatenate([jnp.concatenate(t[low:high], 0) for t in ts], 1)
            score[low * 2 * chunk : high * 2 * chunk, :] += dot(left_side, y, NT)

    groups = 3 * rots
    slabs = [score[i * chunk : (i + 1) * chunk, :] * (2.0 / band) for i in range(groups)]
    highest = functools.reduce(jnp.maximum, slabs)
    low = -3.0e38

    def over_shifts(op, row):
        joined = op(op(row[:, :count], row[:, count : 2 * count]), row[:, 2 * count :])
        return joined, jnp.concatenate([joined] * 3, 1)

    theirs = x_ref[blocks // 2, 2 * rows :, :].astype(jnp.float32)[:2, :own].astype(jnp.int32)
    row_class = lax.broadcasted_iota(jnp.int32, (chunk, 3 * count), 0) + pl.program_id(0) * chunk
    named, tops, wide_tops = [], [], []
    for a in range(2):
        relative = jnp.concatenate([ref[a : a + 1, :] ^ me_ref[0] for ref in (list_ref, theirs)], 1)
        slot = functools.reduce(jnp.add, [((relative >> bit) & 1) << t for t, bit in enumerate(order)])
        slot = jnp.where((relative & 1) == 0, slot, -1)
        named.append(row_class == jnp.concatenate([slot] * 3, 1))
        best = jnp.max(jnp.where(named[a], highest, low), 0, keepdims=True)
        top, wide_top = over_shifts(jnp.maximum, best)
        tops.append(top)
        wide_tops.append(wide_top)
    first, second = named
    either = first | second
    top = jnp.where(first, wide_tops[0], wide_tops[1])
    exps = [jnp.where(either, jnp.exp(jnp.where(either, slab - top, 0.0)), 0.0) for slab in slabs]
    summed = functools.reduce(jnp.add, exps)
    totals = []
    for a in range(2):
        partial = jnp.sum(jnp.where(named[a], summed, 0.0), 0, keepdims=True)
        total, wide_total = over_shifts(jnp.add, partial)
        totals.append(jnp.where(wide_total > 0.0, wide_total, 1.0))
        found = jnp.where(
            total > 0.0, tops[a] + jnp.log(jnp.where(total > 0.0, total, 1.0)) - math.log(rots * SHIFTS), 0.0
        )
        for side in range(2):
            at = (side, slice(a, a + 1))
            old = jnp.where(pl.program_id(0) == 0, 0.0, ev_ref[at])
            ev_ref[at] = found[:, side * own : (side + 1) * own] + old
    total = jnp.where(first, totals[0], totals[1])
    weight[...] = jnp.concatenate([e / total for e in exps], 0).astype(jnp.bfloat16)

    @pl.loop(0, band // group)
    def _(g):
        for k in range(0, group, 2):
            j = g * group + k
            two = []
            for i in range(2):
                gathered = dot(weight[...], shifted[j + i], NN)
                at = pl.ds(pl.multiple_of((j + i) * 8, 8), 8)
                c, s = phase_ref[0, at, :], phase_ref[1, at, :]
                tiled = gathered.reshape(rots // 2, 3, 2, chunk, wide)
                still = tiled[:, 0].reshape(rots, chunk, wide)
                plus = tiled[:, 1:, 0].reshape(rots, chunk, wide)
                minus = tiled[:, 1:, 1].reshape(rots, chunk, wide)
                total, change = plus + minus, plus - minus
                re = still[:, :, :band] + c * total[:, :, :band] - s * change[:, :, band:]
                im = still[:, :, band:] + c * total[:, :, band:] + s * change[:, :, :band]
                two.append((re, im))
            both = [jnp.concatenate([one[q] for one in two], 1).astype(jnp.bfloat16) for q in range(2)]
            for r in range(rots):
                at = pl.ds(pl.multiple_of(r * rows + j * chunk, 16), 2 * chunk)
                work[at, :] = jnp.concatenate([both[0][r], both[1][r]], 1)

    @pl.loop(0, rots // 2)
    def _(g):
        for k in range(2):
            r = g * 2 + k
            at = pl.ds(pl.multiple_of(r * rows, rows), rows)
            turned = dot(work[at, :], diag[r], NN)
            left[0, at, :] = turned[:, :band]
            left[1, at, :] = turned[:, band:]

    for c, (i, k) in enumerate(class_at):
        at = pl.ds(c, rots * band, stride=chunk)
        column = jnp.concatenate([left[0, at, :], left[1, at, :]], 1).astype(jnp.bfloat16)
        turned = dot(rot_t[...], column, NN)
        out_refs[i][k, 0] = turned[:, :band].astype(jnp.bfloat16)
        out_refs[i][k, 1] = turned[:, band:].astype(jnp.bfloat16)


def search(me, lists, classes, rotations, x, order):
    band = classes[0].shape[-1]
    wide = 2 * band
    rots = rotations.shape[0]
    own = lists.shape[1]
    chunk = 8
    n = sum(a.shape[0] for a in classes)
    sizes = [a.shape[0] for a in classes] if n == chunk else [chunk]
    phases = jnp.asarray(shift_tables(band, 2 * band))
    whole = lambda shape: pl.BlockSpec(shape, lambda i: (0,) * len(shape))
    apart = pl.BlockSpec(memory_space=pl.ANY)
    class_blocks = [pl.BlockSpec((size, 2, band, band), lambda i: (i, 0, 0, 0)) for size in sizes]
    *sums, evidence = pl.pallas_call(
        functools.partial(
            search_kernel, rots=rots, chunk=chunk, group=64, order=order, n_classes=len(classes)
        ),
        grid=(n // chunk,),
        out_shape=[jax.ShapeDtypeStruct(a.shape, jnp.bfloat16) for a in classes]
        + [jax.ShapeDtypeStruct((2, 2, own), jnp.float32)],
        in_specs=[
            pl.BlockSpec(memory_space=pltpu.SMEM),
            whole((2, own)),
            whole((rots * band, band)),
            apart,
            apart,
        ]
        + class_blocks,
        out_specs=class_blocks + [whole((2, 2, own))],
        scratch_shapes=[
            pltpu.VMEM((3 * rots * band * chunk, wide), jnp.bfloat16),
            pltpu.VMEM((2, rots * band * chunk, band), jnp.float32),
            pltpu.VMEM((band, 6 * own, wide), jnp.bfloat16),
            pltpu.VMEM((3 * rots * chunk, 6 * own), jnp.float32),
            pltpu.VMEM((rots, wide, wide), jnp.bfloat16),
            pltpu.VMEM((band, rots * band), jnp.bfloat16),
            pltpu.VMEM((3 * rots * chunk, 6 * own), jnp.bfloat16),
            pltpu.VMEM(phases.shape, jnp.float32),
            pltpu.VMEM(x.shape, jnp.bfloat16),
            pltpu.SemaphoreType.DMA,
            pltpu.SemaphoreType.DMA,
        ],
        compiler_params=pltpu.CompilerParams(vmem_limit_bytes=(51 if n == chunk else 62) * MIB),
        cost_estimate=pl.CostEstimate(flops=10**10, bytes_accessed=10**7, transcendentals=0),
        name="search",
    )(me, lists, rotations.reshape(rots * band, band), phases, x, *classes)
    return sums, evidence


def rounds(n):
    bits = list(range(n.bit_length() - 2, 0, -1))
    return [tuple(bits[i : i + 2]) for i in range(0, len(bits), 2)]


def masks(bits):
    count = len(bits)
    return [sum(((i >> t) & 1) << bits[count - 1 - t] for t in range(count)) for i in range(1, 1 << count)]


def swap(value, mask, n):
    return lax.ppermute(value, "cls", [(i, i ^ mask) for i in range(n)])


def on_device(tiles, class_lists, offsets, defocus_groups, contrast_table, references, rotations):
    n = lax.axis_size("cls")
    me = jnp.full((1,), lax.axis_index("cls"), jnp.int32)
    box = tiles.shape[-1]
    band = references.shape[-1]
    plan = rounds(n)
    order = [bit for bits in plan for bit in reversed(bits)]

    mine = references.astype(jnp.bfloat16)
    lists = class_lists.T
    shifts = offsets.T
    table = jnp.asarray(fourier_table(box, band))
    blocks = tiles.shape[0] // 8

    near = masks(plan[0])
    if len(plan) == 2 and len(plan[1]) == 1:
        across = masks(plan[1])[0]
        others = [swap(mine, mask, n) for mask in near]
        x0 = spectra(tiles, shifts, lists, defocus_groups, table, contrast_table, 0, blocks)
        others, x0 = lax.optimization_barrier((others, x0))
        mine = jnp.concatenate([mine] + others, 0)
        classes = [mine, swap(mine, across, n)]
    else:
        x0 = spectra(tiles, shifts, lists, defocus_groups, table, contrast_table, 0, blocks)
        for bits in plan:
            mine = jnp.concatenate([mine] + [swap(mine, mask, n) for mask in masks(bits)], 0)
        classes = [mine]
    x = jnp.concatenate([x0, swap(x0, 1, n)], 0)

    sums, evidence = search(me, lists, classes, rotations, x, order)

    evidence = evidence[0] + swap(evidence[1], 1, n)
    if len(classes) == 2:
        (mine, others), (facing, given) = [(part[:1], part[1:]) for part in sums]
        arrived = swap(given, across, n)
        facing, arrived = lax.optimization_barrier((facing, arrived))
        others = (others.astype(jnp.float32) + arrived.astype(jnp.float32)).astype(jnp.bfloat16)
        got = [swap(part, mask, n) for part, mask in zip(jnp.split(others, len(near), 0), near)]
        got.append(swap(facing, across, n))
        sums = functools.reduce(jnp.add, [part.astype(jnp.float32) for part in [mine] + got])
    else:
        sums = sums[0]
        for bits in reversed(plan):
            parts = jnp.split(sums.astype(jnp.bfloat16), 1 << len(bits), 0)
            got = [swap(part, mask, n) for part, mask in zip(parts[1:], masks(bits))]
            sums = functools.reduce(jnp.add, [part.astype(jnp.float32) for part in parts[:1] + got])
    return sums, evidence.T


def solution(mesh):
    return jax.shard_map(
        on_device,
        mesh=mesh,
        in_specs=(
            P(("groups", "cls"), None, None),
            P(("groups", "cls"), None),
            P(("groups", "cls"), None),
            P(("groups", "cls")),
            P(),
            P(("groups", "cls"), None, None, None),
            P(),
        ),
        out_specs=(P(("groups", "cls"), None, None, None), P(("groups", "cls"), None)),
        check_vma=False,
    )
```

```python
import functools
import math

import jax
import jax.numpy as jnp
import numpy as np
from jax import lax
from jax.experimental import pallas as pl
from jax.experimental.pallas import tpu as pltpu
from jax.sharding import PartitionSpec as P

SHIFTS = 9
MIB = 1 << 20

NT = (((1,), (1,)), ((), ()))
NN = (((1,), (0,)), ((), ()))


def dot(left, right, dims):
    return lax.dot_general(left, right, dims, preferred_element_type=jnp.float32)


def signed_frequencies(band):
    counter = np.arange(band)
    return np.where(counter < band // 2, counter, counter - band)


def fourier_table(box, band):
    angles = (signed_frequencies(band)[:, None] * np.arange(box)[None, :] % box) * (2.0 * math.pi / box)
    both = np.concatenate([np.cos(angles), np.sin(angles)], 0) / math.sqrt(box)
    return both.astype(np.float32).astype(jnp.bfloat16)


def shift_tables(band, box):
    angles = signed_frequencies(band) * (2.0 * math.pi / box)
    both = []
    for values in (np.cos(angles), np.sin(angles)):
        by_row = np.repeat(np.broadcast_to(values[:, None], (band, band)), 8, 0)
        both.append(np.concatenate([by_row, np.broadcast_to(values[None, :], (8, band))], 0))
    return np.stack(both).astype(np.float32)


def cos_sin(steps, box):
    quarter = box // 4
    moved = (steps + quarter // 2) & (box - 1)
    turn = moved // quarter
    angle = ((moved & (quarter - 1)) - quarter // 2).astype(jnp.float32) * (2.0 * math.pi / box)
    sq = angle * angle
    c = 1.0 + sq * (-1 / 2 + sq * (1 / 24 + sq * (-1 / 720 + sq * (1 / 40320))))
    s = angle * (1.0 + sq * (-1 / 6 + sq * (1 / 120 + sq * (-1 / 5040 + sq * (1 / 362880)))))
    odd = (turn & 1) == 1
    cosine = jnp.where(odd, s, c)
    sine = jnp.where(odd, c, s)
    cosine = jnp.where((turn == 1) | (turn == 2), -cosine, cosine)
    sine = jnp.where(turn >= 2, -sine, sine)
    return cosine, sine


def iota_frequency(shape, dim):
    band = shape[dim]
    counter = lax.broadcasted_iota(jnp.int32, shape, dim)
    return jnp.where(counter < band // 2, counter, counter - band)


def spectra_kernel(grp_ref, off_ref, list_ref, tile_ref, table_ref, contrast_ref, out_ref, stage, *, block, start):
    box = tile_ref.shape[-1]
    band = contrast_ref.shape[-1]
    first = (pl.program_id(0) + start) * block
    table = table_ref[...]
    count = off_ref.shape[1]
    lane = lax.broadcasted_iota(jnp.int32, (block, count), 1)
    place = lax.broadcasted_iota(jnp.int32, (block, count), 0) + first
    row_shift = jnp.sum(jnp.where(lane == place, off_ref[0:1, :], 0), 1, keepdims=True)
    col_shift = jnp.sum(jnp.where(lane == place, off_ref[1:2, :], 0), 1, keepdims=True)
    diagonal = lax.broadcasted_iota(jnp.int32, (block, block), 0) == lax.broadcasted_iota(
        jnp.int32, (block, block), 1
    )
    row_shift = jnp.sum(jnp.where(diagonal, row_shift, 0), 0, keepdims=True)
    row_cos, row_sin = cos_sin(iota_frequency((band, block), 0) * row_shift, box)
    col_cos, col_sin = cos_sin(iota_frequency((block, band), 1) * col_shift, box)
    for i in range(block):
        first_pass = dot(tile_ref[i], table, NT).astype(jnp.bfloat16)
        second = dot(table, first_pass, NN)
        re = (second[:band, :band] - second[band:, band:]).astype(jnp.bfloat16).astype(jnp.float32)
        im = (-(second[band:, :band] + second[:band, band:])).astype(jnp.bfloat16).astype(jnp.float32)
        rc = jnp.broadcast_to(row_cos[:, i : i + 1], (band, band))
        rs = jnp.broadcast_to(row_sin[:, i : i + 1], (band, band))
        cc, cs = col_cos[i : i + 1], col_sin[i : i + 1]
        gain = contrast_ref[grp_ref[first + i]].astype(jnp.float32)
        c = gain * (rc * cc - rs * cs)
        s = gain * (rs * cc + rc * cs)
        out_re = (c * re - s * im).astype(jnp.bfloat16).astype(jnp.float32)
        out_im = (c * im + s * re).astype(jnp.bfloat16).astype(jnp.float32)
        stage[0, pl.ds(i, band, stride=block), :] = out_re
        stage[1, pl.ds(i, band, stride=block), :] = out_im
    both = jnp.concatenate([stage[q].reshape(band, block, band) for q in range(2)], 1)
    out_ref[0, : band * 2 * block, :] = both.reshape(band * 2 * block, band).astype(jnp.bfloat16)
    lists = jnp.concatenate([list_ref[...].astype(jnp.float32), jnp.zeros((14, count), jnp.float32)], 0)
    lists = jnp.concatenate([lists, jnp.zeros((16, band - count), jnp.float32)], 1)
    out_ref[0, band * 2 * block :, :] = lists.astype(jnp.bfloat16)


def spectra(tiles, shifts, lists, groups, table, contrast, start, blocks):
    _, box, _ = tiles.shape
    band = contrast.shape[-1]
    block = 8
    count = blocks * block
    return pl.pallas_call(
        functools.partial(spectra_kernel, block=block, start=start),
        grid=(blocks,),
        out_shape=jax.ShapeDtypeStruct((blocks, band * 2 * block + 16, band), jnp.bfloat16),
        in_specs=[
            pl.BlockSpec(memory_space=pltpu.SMEM),
            pl.BlockSpec(shifts.shape, lambda i: (0, 0)),
            pl.BlockSpec(lists.shape, lambda i: (0, 0)),
            pl.BlockSpec((block, box, box), lambda i: (i + start, 0, 0)),
            pl.BlockSpec(table.shape, lambda i: (0, 0)),
            pl.BlockSpec(contrast.shape, lambda i: (0, 0, 0)),
        ],
        out_specs=pl.BlockSpec((1, band * 2 * block + 16, band), lambda i: (i, 0, 0)),
        scratch_shapes=[pltpu.VMEM((2, band * block, band), jnp.float32)],
        compiler_params=pltpu.CompilerParams(vmem_limit_bytes=62 * MIB),
        cost_estimate=pl.CostEstimate(
            flops=count * 4 * box**3, bytes_accessed=count * (box * box * 2 + band * band * 4), transcendentals=0
        ),
        name="spectra",
    )(groups, shifts, lists, tiles, table, contrast)


def search_kernel(
    me_ref, list_ref, rot_ref, phase_hbm, x_hbm, *refs, rots, chunk, group, order, n_classes,
):
    class_refs, refs = refs[:n_classes], refs[n_classes:]
    out_refs, refs = refs[:n_classes], refs[n_classes:]
    ev_ref, work, left, shifted, score, diag, rot_t, weight, phase_ref, x_ref, phase_sem, x_sem = refs
    band = rot_ref.shape[-1]
    wide = 2 * band
    own = list_ref.shape[1]
    count = 2 * own
    rows = band * chunk
    class_at = [(i, k) for i, ref in enumerate(class_refs) for k in range(ref.shape[0])]

    phase_copy = pltpu.make_async_copy(phase_hbm, phase_ref, phase_sem)
    x_copy = pltpu.make_async_copy(x_hbm, x_ref, x_sem)
    blocks = x_ref.shape[0]

    @pl.when(pl.program_id(0) == 0)
    def _():
        phase_copy.start()
        x_copy.start()
        diag[...] = jnp.zeros_like(diag)
        for r in range(rots):
            block = rot_ref[r * band : (r + 1) * band, :]
            diag[r, :band, :band] = block
            diag[r, band:, band:] = block
            rot_t[:, r * band : (r + 1) * band] = block.astype(jnp.float32).T.astype(jnp.bfloat16)

    for c, (i, k) in enumerate(class_at):
        both = jnp.concatenate([class_refs[i][k, 0], class_refs[i][k, 1]], 1)
        halfway = dot(rot_ref[...], both, NN)
        at = pl.ds(c, rots * band, stride=chunk)
        left[0, at, :] = halfway[:, :band]
        left[1, at, :] = halfway[:, band:]

    @pl.when(pl.program_id(0) == 0)
    def _():
        phase_copy.wait()

    def paired(one, other):
        joined = [
            jnp.concatenate([half[q].reshape(band, chunk, band) for half in (one, other)], 1)
            .reshape(2 * rows, band)
            .astype(jnp.bfloat16)
            for q in range(2)
        ]
        return jnp.concatenate(joined, 1)

    @pl.loop(0, rots // 2, unroll=3)
    def _(g):
        def place(t):
            return pl.ds(pl.multiple_of((g * 3 + t) * 2 * rows, 2 * rows), 2 * rows)

        still = []
        for k in range(2):
            r = g * 2 + k
            at = pl.ds(pl.multiple_of(r * rows, rows), rows)
            source = jnp.concatenate([left[0, at, :], left[1, at, :]], 1).astype(jnp.bfloat16)
            rotated = dot(source, diag[r], NT)
            re, im = rotated[:, :band], rotated[:, band:]
            c, s = phase_ref[0, :rows, :], phase_ref[1, :rows, :]
            cr, ci, sr, si = c * re, c * im, s * re, s * im
            work[place(1 + k), :] = paired((cr + si, ci - sr), (cr - si, ci + sr))
            still.append((re, im))
        work[place(0), :] = paired(*still)

    @pl.when(pl.program_id(0) == 0)
    def _():
        x_copy.wait()

    score[...] = jnp.zeros_like(score)

    @pl.loop(0, band // group)
    def _(g):
        ys, ts = [], []
        for k in range(group):
            j = g * group + k
            at = pl.ds(pl.multiple_of(j * 16, 16), 16)
            pairs = [x_ref[b, at, :].astype(jnp.float32) for b in range(blocks)]
            re = jnp.concatenate([pair[:8] for pair in pairs], 0)
            im = jnp.concatenate([pair[8:] for pair in pairs], 0)
            c, s = phase_ref[0, rows : rows + 1, :], phase_ref[1, rows : rows + 1, :]
            cr, ci, sr, si = c * re, c * im, s * re, s * im
            y = jnp.concatenate(
                [jnp.concatenate(v, 1) for v in ((re, im), (cr - si, ci + sr), (cr + si, ci - sr))], 0
            ).astype(jnp.bfloat16)
            shifted[j] = y
            ys.append(y)
            tiles = [pl.ds(pl.multiple_of(r * 2 * rows + j * 2 * chunk, 16), 2 * chunk) for r in range(3 * rots // 2)]
            ts.append([work[at, :] for at in tiles])
        y = jnp.concatenate(ys, 1)
        cut = 3 * rots // 4
        for low, high in ((0, cut), (cut, 3 * rots // 2)):
            left_side = jnp.concatenate([jnp.concatenate(t[low:high], 0) for t in ts], 1)
            score[low * 2 * chunk : high * 2 * chunk, :] += dot(left_side, y, NT)

    groups = 3 * rots
    slabs = [score[i * chunk : (i + 1) * chunk, :] * (2.0 / band) for i in range(groups)]
    highest = functools.reduce(jnp.maximum, slabs)
    low = -3.0e38

    def over_shifts(op, row):
        joined = op(op(row[:, :count], row[:, count : 2 * count]), row[:, 2 * count :])
        return joined, jnp.concatenate([joined] * 3, 1)

    theirs = x_ref[blocks // 2, 2 * rows :, :].astype(jnp.float32)[:2, :own].astype(jnp.int32)
    row_class = lax.broadcasted_iota(jnp.int32, (chunk, 3 * count), 0) + pl.program_id(0) * chunk
    named, tops, wide_tops = [], [], []
    for a in range(2):
        relative = jnp.concatenate([ref[a : a + 1, :] ^ me_ref[0] for ref in (list_ref, theirs)], 1)
        slot = functools.reduce(jnp.add, [((relative >> bit) & 1) << t for t, bit in enumerate(order)])
        slot = jnp.where((relative & 1) == 0, slot, -1)
        named.append(row_class == jnp.concatenate([slot] * 3, 1))
        best = jnp.max(jnp.where(named[a], highest, low), 0, keepdims=True)
        top, wide_top = over_shifts(jnp.maximum, best)
        tops.append(top)
        wide_tops.append(wide_top)
    first, second = named
    either = first | second
    top = jnp.where(first, wide_tops[0], wide_tops[1])
    exps = [jnp.where(either, jnp.exp(jnp.where(either, slab - top, 0.0)), 0.0) for slab in slabs]
    summed = functools.reduce(jnp.add, exps)
    totals = []
    for a in range(2):
        partial = jnp.sum(jnp.where(named[a], summed, 0.0), 0, keepdims=True)
        total, wide_total = over_shifts(jnp.add, partial)
        totals.append(jnp.where(wide_total > 0.0, wide_total, 1.0))
        found = jnp.where(
            total > 0.0, tops[a] + jnp.log(jnp.where(total > 0.0, total, 1.0)) - math.log(rots * SHIFTS), 0.0
        )
        for side in range(2):
            at = (side, slice(a, a + 1))
            old = jnp.where(pl.program_id(0) == 0, 0.0, ev_ref[at])
            ev_ref[at] = found[:, side * own : (side + 1) * own] + old
    total = jnp.where(first, totals[0], totals[1])
    weight[...] = jnp.concatenate([e / total for e in exps], 0).astype(jnp.bfloat16)

    @pl.loop(0, band // group)
    def _(g):
        for k in range(0, group, 2):
            j = g * group + k
            two = []
            for i in range(2):
                gathered = dot(weight[...], shifted[j + i], NN)
                at = pl.ds(pl.multiple_of((j + i) * 8, 8), 8)
                c, s = phase_ref[0, at, :], phase_ref[1, at, :]
                tiled = gathered.reshape(rots // 2, 3, 2, chunk, wide)
                still = tiled[:, 0].reshape(rots, chunk, wide)
                plus = tiled[:, 1:, 0].reshape(rots, chunk, wide)
                minus = tiled[:, 1:, 1].reshape(rots, chunk, wide)
                total, change = plus + minus, plus - minus
                re = still[:, :, :band] + c * total[:, :, :band] - s * change[:, :, band:]
                im = still[:, :, band:] + c * total[:, :, band:] + s * change[:, :, :band]
                two.append((re, im))
            both = [jnp.concatenate([one[q] for one in two], 1).astype(jnp.bfloat16) for q in range(2)]
            for r in range(rots):
                at = pl.ds(pl.multiple_of(r * rows + j * chunk, 16), 2 * chunk)
                work[at, :] = jnp.concatenate([both[0][r], both[1][r]], 1)

    @pl.loop(0, rots // 2, unroll=3)
    def _(g):
        for k in range(2):
            r = g * 2 + k
            at = pl.ds(pl.multiple_of(r * rows, rows), rows)
            turned = dot(work[at, :], diag[r], NN)
            left[0, at, :] = turned[:, :band]
            left[1, at, :] = turned[:, band:]

    for c, (i, k) in enumerate(class_at):
        at = pl.ds(c, rots * band, stride=chunk)
        column = jnp.concatenate([left[0, at, :], left[1, at, :]], 1).astype(jnp.bfloat16)
        turned = dot(rot_t[...], column, NN)
        out_refs[i][k, 0] = turned[:, :band].astype(jnp.bfloat16)
        out_refs[i][k, 1] = turned[:, band:].astype(jnp.bfloat16)


def search(me, lists, classes, rotations, x, order):
    band = classes[0].shape[-1]
    wide = 2 * band
    rots = rotations.shape[0]
    own = lists.shape[1]
    chunk = 8
    n = sum(a.shape[0] for a in classes)
    sizes = [a.shape[0] for a in classes] if n == chunk else [chunk]
    phases = jnp.asarray(shift_tables(band, 2 * band))
    whole = lambda shape: pl.BlockSpec(shape, lambda i: (0,) * len(shape))
    apart = pl.BlockSpec(memory_space=pl.ANY)
    class_blocks = [pl.BlockSpec((size, 2, band, band), lambda i: (i, 0, 0, 0)) for size in sizes]
    *sums, evidence = pl.pallas_call(
        functools.partial(
            search_kernel, rots=rots, chunk=chunk, group=128, order=order, n_classes=len(classes)
        ),
        grid=(n // chunk,),
        out_shape=[jax.ShapeDtypeStruct(a.shape, jnp.bfloat16) for a in classes]
        + [jax.ShapeDtypeStruct((2, 2, own), jnp.float32)],
        in_specs=[
            pl.BlockSpec(memory_space=pltpu.SMEM),
            whole((2, own)),
            whole((rots * band, band)),
            apart,
            apart,
        ]
        + class_blocks,
        out_specs=class_blocks + [whole((2, 2, own))],
        scratch_shapes=[
            pltpu.VMEM((3 * rots * band * chunk, wide), jnp.bfloat16),
            pltpu.VMEM((2, rots * band * chunk, band), jnp.float32),
            pltpu.VMEM((band, 6 * own, wide), jnp.bfloat16),
            pltpu.VMEM((3 * rots * chunk, 6 * own), jnp.float32),
            pltpu.VMEM((rots, wide, wide), jnp.bfloat16),
            pltpu.VMEM((band, rots * band), jnp.bfloat16),
            pltpu.VMEM((3 * rots * chunk, 6 * own), jnp.bfloat16),
            pltpu.VMEM(phases.shape, jnp.float32),
            pltpu.VMEM(x.shape, jnp.bfloat16),
            pltpu.SemaphoreType.DMA,
            pltpu.SemaphoreType.DMA,
        ],
        compiler_params=pltpu.CompilerParams(vmem_limit_bytes=(51 if n == chunk else 62) * MIB),
        cost_estimate=pl.CostEstimate(flops=10**10, bytes_accessed=10**7, transcendentals=0),
        name="search",
    )(me, lists, rotations.reshape(rots * band, band), phases, x, *classes)
    return sums, evidence


def rounds(n):
    bits = list(range(n.bit_length() - 2, 0, -1))
    return [tuple(bits[i : i + 2]) for i in range(0, len(bits), 2)]


def masks(bits):
    count = len(bits)
    return [sum(((i >> t) & 1) << bits[count - 1 - t] for t in range(count)) for i in range(1, 1 << count)]


def swap(value, mask, n):
    return lax.ppermute(value, "cls", [(i, i ^ mask) for i in range(n)])


def on_device(tiles, class_lists, offsets, defocus_groups, contrast_table, references, rotations):
    n = lax.axis_size("cls")
    me = jnp.full((1,), lax.axis_index("cls"), jnp.int32)
    box = tiles.shape[-1]
    band = references.shape[-1]
    plan = rounds(n)
    order = [bit for bits in plan for bit in reversed(bits)]

    mine = references.astype(jnp.bfloat16)
    lists = class_lists.T
    shifts = offsets.T
    table = jnp.asarray(fourier_table(box, band))
    blocks = tiles.shape[0] // 8

    near = masks(plan[0])
    if len(plan) == 2 and len(plan[1]) == 1:
        across = masks(plan[1])[0]
        others = [swap(mine, mask, n) for mask in near]
        x0 = spectra(tiles, shifts, lists, defocus_groups, table, contrast_table, 0, blocks)
        others, x0 = lax.optimization_barrier((others, x0))
        mine = jnp.concatenate([mine] + others, 0)
        classes = [mine, swap(mine, across, n)]
    else:
        x0 = spectra(tiles, shifts, lists, defocus_groups, table, contrast_table, 0, blocks)
        for bits in plan:
            mine = jnp.concatenate([mine] + [swap(mine, mask, n) for mask in masks(bits)], 0)
        classes = [mine]
    x = jnp.concatenate([x0, swap(x0, 1, n)], 0)

    sums, evidence = search(me, lists, classes, rotations, x, order)

    evidence = evidence[0] + swap(evidence[1], 1, n)
    if len(classes) == 2:
        arrived = swap(sums[1], across, n)
        joined = sums[0].astype(jnp.float32) + arrived.astype(jnp.float32)
        mine, *parts = jnp.split(joined, 1 + len(near), 0)
        got = [swap(part.astype(jnp.bfloat16), mask, n) for part, mask in zip(parts, near)]
        sums = functools.reduce(jnp.add, [part.astype(jnp.float32) for part in [mine] + got])
    else:
        sums = sums[0]
        for bits in reversed(plan):
            parts = jnp.split(sums.astype(jnp.bfloat16), 1 << len(bits), 0)
            got = [swap(part, mask, n) for part, mask in zip(parts[1:], masks(bits))]
            sums = functools.reduce(jnp.add, [part.astype(jnp.float32) for part in parts[:1] + got])
    return sums, evidence.T


def solution(mesh):
    return jax.shard_map(
        on_device,
        mesh=mesh,
        in_specs=(
            P(("groups", "cls"), None, None),
            P(("groups", "cls"), None),
            P(("groups", "cls"), None),
            P(("groups", "cls")),
            P(),
            P(("groups", "cls"), None, None, None),
            P(),
        ),
        out_specs=(P(("groups", "cls"), None, None, None), P(("groups", "cls"), None)),
        check_vma=False,
    )
```

```python
import functools
import math

import jax
import jax.numpy as jnp
import numpy as np
from jax import lax
from jax.experimental import pallas as pl
from jax.experimental.pallas import tpu as pltpu
from jax.sharding import PartitionSpec as P

SHIFTS = 9
MIB = 1 << 20

NT = (((1,), (1,)), ((), ()))
NN = (((1,), (0,)), ((), ()))


def dot(left, right, dims):
    return lax.dot_general(left, right, dims, preferred_element_type=jnp.float32)


def signed_frequencies(band):
    counter = np.arange(band)
    return np.where(counter < band // 2, counter, counter - band)


def fourier_table(box, band):
    angles = (signed_frequencies(band)[:, None] * np.arange(box)[None, :] % box) * (2.0 * math.pi / box)
    both = np.concatenate([np.cos(angles), np.sin(angles)], 0) / math.sqrt(box)
    return np.stack([both, both.T]).astype(np.float32).astype(jnp.bfloat16)


def shift_tables(band, box):
    angles = signed_frequencies(band) * (2.0 * math.pi / box)
    both = []
    for values in (np.cos(angles), np.sin(angles)):
        by_row = np.repeat(np.broadcast_to(values[:, None], (band, band)), 8, 0)
        both.append(np.concatenate([by_row, np.broadcast_to(values[None, :], (8, band))], 0))
    return np.stack(both).astype(np.float32)


def cos_sin(steps, box):
    quarter = box // 4
    moved = (steps + quarter // 2) & (box - 1)
    turn = moved // quarter
    angle = ((moved & (quarter - 1)) - quarter // 2).astype(jnp.float32) * (2.0 * math.pi / box)
    sq = angle * angle
    c = 1.0 + sq * (-1 / 2 + sq * (1 / 24 + sq * (-1 / 720 + sq * (1 / 40320))))
    s = angle * (1.0 + sq * (-1 / 6 + sq * (1 / 120 + sq * (-1 / 5040 + sq * (1 / 362880)))))
    odd = (turn & 1) == 1
    cosine = jnp.where(odd, s, c)
    sine = jnp.where(odd, c, s)
    cosine = jnp.where((turn == 1) | (turn == 2), -cosine, cosine)
    sine = jnp.where(turn >= 2, -sine, sine)
    return cosine, sine


def iota_frequency(shape, dim):
    band = shape[dim]
    counter = lax.broadcasted_iota(jnp.int32, shape, dim)
    return jnp.where(counter < band // 2, counter, counter - band)


def spectra_kernel(grp_ref, off_ref, list_ref, tile_ref, table_ref, contrast_ref, out_ref, stage, *, block, start):
    box = tile_ref.shape[-1]
    band = contrast_ref.shape[-1]
    first = (pl.program_id(0) + start) * block
    table, table_t = table_ref[0], table_ref[1]
    count = off_ref.shape[1]
    lane = lax.broadcasted_iota(jnp.int32, (block, count), 1)
    place = lax.broadcasted_iota(jnp.int32, (block, count), 0) + first
    row_shift = jnp.sum(jnp.where(lane == place, off_ref[0:1, :], 0), 1, keepdims=True)
    col_shift = jnp.sum(jnp.where(lane == place, off_ref[1:2, :], 0), 1, keepdims=True)
    diagonal = lax.broadcasted_iota(jnp.int32, (block, block), 0) == lax.broadcasted_iota(
        jnp.int32, (block, block), 1
    )
    row_shift = jnp.sum(jnp.where(diagonal, row_shift, 0), 0, keepdims=True)
    row_cos, row_sin = cos_sin(iota_frequency((band, block), 0) * row_shift, box)
    col_cos, col_sin = cos_sin(iota_frequency((block, band), 1) * col_shift, box)
    for i in range(block):
        first_pass = dot(tile_ref[i], table_t, NN).astype(jnp.bfloat16)
        second = dot(table, first_pass, NN)
        re = (second[:band, :band] - second[band:, band:]).astype(jnp.bfloat16).astype(jnp.float32)
        im = (-(second[band:, :band] + second[:band, band:])).astype(jnp.bfloat16).astype(jnp.float32)
        rc = jnp.broadcast_to(row_cos[:, i : i + 1], (band, band))
        rs = jnp.broadcast_to(row_sin[:, i : i + 1], (band, band))
        cc, cs = col_cos[i : i + 1], col_sin[i : i + 1]
        gain = contrast_ref[grp_ref[first + i]].astype(jnp.float32)
        c = gain * (rc * cc - rs * cs)
        s = gain * (rs * cc + rc * cs)
        out_re = (c * re - s * im).astype(jnp.bfloat16).astype(jnp.float32)
        out_im = (c * im + s * re).astype(jnp.bfloat16).astype(jnp.float32)
        stage[0, pl.ds(i, band, stride=block), :] = out_re
        stage[1, pl.ds(i, band, stride=block), :] = out_im
    both = jnp.concatenate([stage[q, : band * block, :].reshape(band, block, band) for q in range(2)], 1)
    out_ref[0, : band * 2 * block, :] = both.reshape(band * 2 * block, band).astype(jnp.bfloat16)
    lists = jnp.concatenate([list_ref[...].astype(jnp.float32), jnp.zeros((14, count), jnp.float32)], 0)
    lists = jnp.concatenate([lists, jnp.zeros((16, band - count), jnp.float32)], 1)
    out_ref[0, band * 2 * block :, :] = lists.astype(jnp.bfloat16)


def spectra(tiles, shifts, lists, groups, table, contrast, start, blocks):
    _, box, _ = tiles.shape
    band = contrast.shape[-1]
    block = 8
    count = blocks * block
    return pl.pallas_call(
        functools.partial(spectra_kernel, block=block, start=start),
        grid=(blocks,),
        out_shape=jax.ShapeDtypeStruct((blocks, band * 2 * block + 16, band), jnp.bfloat16),
        in_specs=[
            pl.BlockSpec(memory_space=pltpu.SMEM),
            pl.BlockSpec(shifts.shape, lambda i: (0, 0)),
            pl.BlockSpec(lists.shape, lambda i: (0, 0)),
            pl.BlockSpec((block, box, box), lambda i: (i + start, 0, 0)),
            pl.BlockSpec(table.shape, lambda i: (0, 0, 0)),
            pl.BlockSpec(contrast.shape, lambda i: (0, 0, 0)),
        ],
        out_specs=pl.BlockSpec((1, band * 2 * block + 16, band), lambda i: (i, 0, 0)),
        scratch_shapes=[pltpu.VMEM((2, band * block + 8, band), jnp.float32)],
        compiler_params=pltpu.CompilerParams(vmem_limit_bytes=62 * MIB),
        cost_estimate=pl.CostEstimate(
            flops=count * 4 * box**3, bytes_accessed=count * (box * box * 2 + band * band * 4), transcendentals=0
        ),
        name="spectra",
    )(groups, shifts, lists, tiles, table, contrast)


def search_kernel(
    me_ref, list_ref, rot_ref, phase_hbm, x_hbm, *refs, rots, chunk, group, order, n_classes,
):
    class_refs, refs = refs[:n_classes], refs[n_classes:]
    out_refs, refs = refs[:n_classes], refs[n_classes:]
    ev_ref, work, left, shifted, score, diag, rot_t, weight, phase_ref, x_ref, phase_sem, x_sem = refs
    band = rot_ref.shape[-1]
    wide = 2 * band
    own = list_ref.shape[1]
    count = 2 * own
    rows = band * chunk
    class_at = [(i, k) for i, ref in enumerate(class_refs) for k in range(ref.shape[0])]

    phase_copy = pltpu.make_async_copy(phase_hbm, phase_ref, phase_sem)
    x_copy = pltpu.make_async_copy(x_hbm, x_ref, x_sem)
    blocks = x_ref.shape[0]

    @pl.when(pl.program_id(0) == 0)
    def _():
        phase_copy.start()
        x_copy.start()
        diag[...] = jnp.zeros_like(diag)
        for r in range(rots):
            block = rot_ref[r * band : (r + 1) * band, :]
            diag[r, :band, :band] = block
            diag[r, band:, band:] = block
            rot_t[:, r * band : (r + 1) * band] = block.astype(jnp.float32).T.astype(jnp.bfloat16)

    for c, (i, k) in enumerate(class_at):
        both = jnp.concatenate([class_refs[i][k, 0], class_refs[i][k, 1]], 1)
        halfway = dot(rot_ref[...], both, NN)
        at = pl.ds(c, rots * band, stride=chunk)
        left[0, at, :] = halfway[:, :band]
        left[1, at, :] = halfway[:, band:]

    @pl.when(pl.program_id(0) == 0)
    def _():
        phase_copy.wait()

    def paired(one, other):
        joined = [
            jnp.concatenate([half[q].reshape(band, chunk, band) for half in (one, other)], 1)
            .reshape(2 * rows, band)
            .astype(jnp.bfloat16)
            for q in range(2)
        ]
        return jnp.concatenate(joined, 1)

    @pl.loop(0, rots // 2, unroll=3)
    def _(g):
        def place(t):
            return pl.ds(pl.multiple_of((g * 3 + t) * 2 * rows, 2 * rows), 2 * rows)

        still = []
        for k in range(2):
            r = g * 2 + k
            at = pl.ds(pl.multiple_of(r * rows, rows), rows)
            source = jnp.concatenate([left[0, at, :], left[1, at, :]], 1).astype(jnp.bfloat16)
            rotated = dot(source, diag[r], NT)
            re, im = rotated[:, :band], rotated[:, band:]
            c, s = phase_ref[0, :rows, :], phase_ref[1, :rows, :]
            cr, ci, sr, si = c * re, c * im, s * re, s * im
            work[place(1 + k), :] = paired((cr + si, ci - sr), (cr - si, ci + sr))
            still.append((re, im))
        work[place(0), :] = paired(*still)

    @pl.when(pl.program_id(0) == 0)
    def _():
        x_copy.wait()

    score[...] = jnp.zeros_like(score)

    @pl.loop(0, band // group)
    def _(g):
        ys, ts = [], []
        for k in range(group):
            j = g * group + k
            at = pl.ds(pl.multiple_of(j * 16, 16), 16)
            pairs = [x_ref[b, at, :].astype(jnp.float32) for b in range(blocks)]
            re = jnp.concatenate([pair[:8] for pair in pairs], 0)
            im = jnp.concatenate([pair[8:] for pair in pairs], 0)
            c, s = phase_ref[0, rows : rows + 1, :], phase_ref[1, rows : rows + 1, :]
            cr, ci, sr, si = c * re, c * im, s * re, s * im
            y = jnp.concatenate(
                [jnp.concatenate(v, 1) for v in ((re, im), (cr - si, ci + sr), (cr + si, ci - sr))], 0
            ).astype(jnp.bfloat16)
            shifted[j] = y
            ys.append(y)
            tiles = [pl.ds(pl.multiple_of(r * 2 * rows + j * 2 * chunk, 16), 2 * chunk) for r in range(3 * rots // 2)]
            ts.append([work[at, :] for at in tiles])
        y = jnp.concatenate(ys, 1)
        cut = 3 * rots // 4
        for low, high in ((0, cut), (cut, 3 * rots // 2)):
            left_side = jnp.concatenate([jnp.concatenate(t[low:high], 0) for t in ts], 1)
            score[low * 2 * chunk : high * 2 * chunk, :] += dot(left_side, y, NT)

    groups = 3 * rots
    slabs = [score[i * chunk : (i + 1) * chunk, :] * (2.0 / band) for i in range(groups)]
    highest = functools.reduce(jnp.maximum, slabs)
    low = -3.0e38

    def over_shifts(op, row):
        joined = op(op(row[:, :count], row[:, count : 2 * count]), row[:, 2 * count :])
        return joined, jnp.concatenate([joined] * 3, 1)

    theirs = x_ref[blocks // 2, 2 * rows :, :].astype(jnp.float32)[:2, :own].astype(jnp.int32)
    row_class = lax.broadcasted_iota(jnp.int32, (chunk, 3 * count), 0) + pl.program_id(0) * chunk
    named, tops, wide_tops = [], [], []
    for a in range(2):
        relative = jnp.concatenate([ref[a : a + 1, :] ^ me_ref[0] for ref in (list_ref, theirs)], 1)
        slot = functools.reduce(jnp.add, [((relative >> bit) & 1) << t for t, bit in enumerate(order)])
        slot = jnp.where((relative & 1) == 0, slot, -1)
        named.append(row_class == jnp.concatenate([slot] * 3, 1))
        best = jnp.max(jnp.where(named[a], highest, low), 0, keepdims=True)
        top, wide_top = over_shifts(jnp.maximum, best)
        tops.append(top)
        wide_tops.append(wide_top)
    first, second = named
    either = first | second
    top = jnp.where(first, wide_tops[0], wide_tops[1])
    exps = [jnp.where(either, jnp.exp(jnp.where(either, slab - top, 0.0)), 0.0) for slab in slabs]
    summed = functools.reduce(jnp.add, exps)
    totals = []
    for a in range(2):
        partial = jnp.sum(jnp.where(named[a], summed, 0.0), 0, keepdims=True)
        total, wide_total = over_shifts(jnp.add, partial)
        totals.append(jnp.where(wide_total > 0.0, wide_total, 1.0))
        found = jnp.where(
            total > 0.0, tops[a] + jnp.log(jnp.where(total > 0.0, total, 1.0)) - math.log(rots * SHIFTS), 0.0
        )
        for side in range(2):
            at = (side, slice(a, a + 1))
            old = jnp.where(pl.program_id(0) == 0, 0.0, ev_ref[at])
            ev_ref[at] = found[:, side * own : (side + 1) * own] + old
    total = jnp.where(first, totals[0], totals[1])
    weight[...] = jnp.concatenate([e / total for e in exps], 0).astype(jnp.bfloat16)

    @pl.loop(0, band // group)
    def _(g):
        for k in range(0, group, 2):
            j = g * group + k
            two = []
            for i in range(2):
                gathered = dot(weight[...], shifted[j + i], NN)
                at = pl.ds(pl.multiple_of((j + i) * 8, 8), 8)
                c, s = phase_ref[0, at, :], phase_ref[1, at, :]
                tiled = gathered.reshape(rots // 2, 3, 2, chunk, wide)
                still = tiled[:, 0].reshape(rots, chunk, wide)
                plus = tiled[:, 1:, 0].reshape(rots, chunk, wide)
                minus = tiled[:, 1:, 1].reshape(rots, chunk, wide)
                total, change = plus + minus, plus - minus
                re = still[:, :, :band] + c * total[:, :, :band] - s * change[:, :, band:]
                im = still[:, :, band:] + c * total[:, :, band:] + s * change[:, :, :band]
                two.append((re, im))
            both = [jnp.concatenate([one[q] for one in two], 1).astype(jnp.bfloat16) for q in range(2)]
            for r in range(rots):
                at = pl.ds(pl.multiple_of(r * rows + j * chunk, 16), 2 * chunk)
                work[at, :] = jnp.concatenate([both[0][r], both[1][r]], 1)

    @pl.loop(0, rots // 2, unroll=3)
    def _(g):
        for k in range(2):
            r = g * 2 + k
            at = pl.ds(pl.multiple_of(r * rows, rows), rows)
            turned = dot(work[at, :], diag[r], NN)
            left[0, at, :] = turned[:, :band]
            left[1, at, :] = turned[:, band:]

    for c, (i, k) in enumerate(class_at):
        at = pl.ds(c, rots * band, stride=chunk)
        column = jnp.concatenate([left[0, at, :], left[1, at, :]], 1).astype(jnp.bfloat16)
        turned = dot(rot_t[...], column, NN)
        out_refs[i][k, 0] = turned[:, :band].astype(jnp.bfloat16)
        out_refs[i][k, 1] = turned[:, band:].astype(jnp.bfloat16)


def search(me, lists, classes, rotations, x, order):
    band = classes[0].shape[-1]
    wide = 2 * band
    rots = rotations.shape[0]
    own = lists.shape[1]
    chunk = 8
    n = sum(a.shape[0] for a in classes)
    sizes = [a.shape[0] for a in classes] if n == chunk else [chunk]
    phases = jnp.asarray(shift_tables(band, 2 * band))
    whole = lambda shape: pl.BlockSpec(shape, lambda i: (0,) * len(shape))
    apart = pl.BlockSpec(memory_space=pl.ANY)
    class_blocks = [pl.BlockSpec((size, 2, band, band), lambda i: (i, 0, 0, 0)) for size in sizes]
    *sums, evidence = pl.pallas_call(
        functools.partial(
            search_kernel, rots=rots, chunk=chunk, group=128, order=order, n_classes=len(classes)
        ),
        grid=(n // chunk,),
        out_shape=[jax.ShapeDtypeStruct(a.shape, jnp.bfloat16) for a in classes]
        + [jax.ShapeDtypeStruct((2, 2, own), jnp.float32)],
        in_specs=[
            pl.BlockSpec(memory_space=pltpu.SMEM),
            whole((2, own)),
            whole((rots * band, band)),
            apart,
            apart,
        ]
        + class_blocks,
        out_specs=class_blocks + [whole((2, 2, own))],
        scratch_shapes=[
            pltpu.VMEM((3 * rots * band * chunk, wide), jnp.bfloat16),
            pltpu.VMEM((2, rots * band * chunk + 8, band), jnp.float32),
            pltpu.VMEM((band, 6 * own, wide), jnp.bfloat16),
            pltpu.VMEM((3 * rots * chunk, 6 * own), jnp.float32),
            pltpu.VMEM((rots, wide, wide), jnp.bfloat16),
            pltpu.VMEM((band, rots * band), jnp.bfloat16),
            pltpu.VMEM((3 * rots * chunk, 6 * own), jnp.bfloat16),
            pltpu.VMEM(phases.shape, jnp.float32),
            pltpu.VMEM(x.shape, jnp.bfloat16),
            pltpu.SemaphoreType.DMA,
            pltpu.SemaphoreType.DMA,
        ],
        compiler_params=pltpu.CompilerParams(vmem_limit_bytes=(51 if n == chunk else 62) * MIB),
        cost_estimate=pl.CostEstimate(flops=10**10, bytes_accessed=10**7, transcendentals=0),
        name="search",
    )(me, lists, rotations.reshape(rots * band, band), phases, x, *classes)
    return sums, evidence


def rounds(n):
    bits = list(range(n.bit_length() - 2, 0, -1))
    return [tuple(bits[i : i + 2]) for i in range(0, len(bits), 2)]


def masks(bits):
    count = len(bits)
    return [sum(((i >> t) & 1) << bits[count - 1 - t] for t in range(count)) for i in range(1, 1 << count)]


def swap(value, mask, n):
    return lax.ppermute(value, "cls", [(i, i ^ mask) for i in range(n)])


def on_device(tiles, class_lists, offsets, defocus_groups, contrast_table, references, rotations):
    n = lax.axis_size("cls")
    me = jnp.full((1,), lax.axis_index("cls"), jnp.int32)
    box = tiles.shape[-1]
    band = references.shape[-1]
    plan = rounds(n)
    order = [bit for bits in plan for bit in reversed(bits)]

    mine = references.astype(jnp.bfloat16)
    lists = class_lists.T
    shifts = offsets.T
    table = jnp.asarray(fourier_table(box, band))
    blocks = tiles.shape[0] // 8

    near = masks(plan[0])
    if len(plan) == 2 and len(plan[1]) == 1:
        across = masks(plan[1])[0]
        others = [swap(mine, mask, n) for mask in near]
        x0 = spectra(tiles, shifts, lists, defocus_groups, table, contrast_table, 0, blocks)
        others, x0 = lax.optimization_barrier((others, x0))
        mine = jnp.concatenate([mine] + others, 0)
        classes = [mine, swap(mine, across, n)]
    else:
        x0 = spectra(tiles, shifts, lists, defocus_groups, table, contrast_table, 0, blocks)
        for bits in plan:
            mine = jnp.concatenate([mine] + [swap(mine, mask, n) for mask in masks(bits)], 0)
        classes = [mine]
    x = jnp.concatenate([x0, swap(x0, 1, n)], 0)

    sums, evidence = search(me, lists, classes, rotations, x, order)

    evidence = evidence[0] + swap(evidence[1], 1, n)
    if len(classes) == 2:
        arrived = swap(sums[1], across, n)
        joined = sums[0].astype(jnp.float32) + arrived.astype(jnp.float32)
        mine, *parts = jnp.split(joined, 1 + len(near), 0)
        got = [swap(part.astype(jnp.bfloat16), mask, n) for part, mask in zip(parts, near)]
        sums = functools.reduce(jnp.add, [part.astype(jnp.float32) for part in [mine] + got])
    else:
        sums = sums[0]
        for bits in reversed(plan):
            parts = jnp.split(sums.astype(jnp.bfloat16), 1 << len(bits), 0)
            got = [swap(part, mask, n) for part, mask in zip(parts[1:], masks(bits))]
            sums = functools.reduce(jnp.add, [part.astype(jnp.float32) for part in parts[:1] + got])
    return sums, evidence.T


def solution(mesh):
    return jax.shard_map(
        on_device,
        mesh=mesh,
        in_specs=(
            P(("groups", "cls"), None, None),
            P(("groups", "cls"), None),
            P(("groups", "cls"), None),
            P(("groups", "cls")),
            P(),
            P(("groups", "cls"), None, None, None),
            P(),
        ),
        out_specs=(P(("groups", "cls"), None, None, None), P(("groups", "cls"), None)),
        check_vma=False,
    )
```
